256 devices in a mesh: vid: 16 (over y_hi, z), seq: 16 (over x, y_lo, core).
Axes of the slice: x: 4, y: 4 (y_hi: 2, y_lo: 2; y = y_hi * 2 + y_lo), z: 8, core: 2. Of those that a mesh axis runs over, the one named last changes fastest.
Arguments:
- video: bfloat16 [16, 512, 4096], P('vid', 'seq'), may hold values from -8 to 8
- video_length: int32 [16], P('vid'), may hold values from 128 to 512
- prompt: bfloat16 [16, 128, 4096], P('vid', 'seq'), may hold values from -6 to 6
- prompt_length: int32 [16], replicated, may hold values from 32 to 128
- prompt_choice: int32 [16], P('vid'), may hold values from 0 to 15
- ffn_gain: float32 [4096], replicated, may hold values from 0.1 to 1.9
- ffn_gate: bfloat16 [4096, 6144], P(None, 'seq'), may hold values from -0.09375 to 0.09375
- ffn_up: bfloat16 [4096, 6144], P(None, 'seq'), may hold values from -0.09375 to 0.09375
- ffn_down: bfloat16 [6144, 4096], P('seq'), may hold values from -0.078125 to 0.078125
- final_gain: float32 [4096], replicated, may hold values from 0.1 to 1.9
- video_gain: float32 [4096], replicated, may hold values from 0.1 to 1.9
- w_query: bfloat16 [4096, 4096], P('vid', 'seq'), may hold values from -1 to 1
- w_key: bfloat16 [4096, 4096], P('vid', 'seq'), may hold values from -3 to 3
- w_value: bfloat16 [4096, 4096], P('vid', 'seq'), may hold values from -0.09375 to 0.09375
- w_text_key: bfloat16 [4096, 4096], P('vid', 'seq'), may hold values from -0.09375 to 0.09375
- w_text_value: bfloat16 [4096, 4096], P('vid', 'seq'), may hold values from -0.09375 to 0.09375
- w_out: bfloat16 [4096, 4096], P('seq', 'vid'), may hold values from -0.09375 to 0.09375
Outputs:
- updated: bfloat16 [16, 512, 4096], P('vid', 'seq')
The draws below stay inside these ranges and needn't reach their ends.
Inputs may be any that keep to these rules, and one draw needn't show every extreme that they name: `prompt_choice`: A prompt may serve several videos or none.
All inputs are finite; a program needn't handle non-finite values.
Results may differ from the reference program's by a relative error of at most 0.0085.
Values may be sent and summed in bfloat16 or wider, within the bound.
A program may use at most 128 MiB of HBM per device.

```python
import jax
import jax.numpy as jnp
from jax import lax

HEADS = 32
HD = 128
D = 4096
DT = 4096
FFT = 6144
LMAX = 512
PLEN = 128
VIDEOS = 16
PROMPTS = 16


def query_draw(key):
    sample = jax.random.normal(jax.random.fold_in(key, 802), (D, D), jnp.float32)
    return jnp.clip(sample, -4.0, 4.0) * D ** (-0.5)


def draw_w_query(key, part):
    result = query_draw(key)
    return result.astype(jnp.bfloat16)


def draw_w_key(key, part):
    sample = jax.random.normal(jax.random.fold_in(key, 803), (D, D), jnp.float32)
    result = jnp.clip(sample, -4.0, 4.0) * D ** (-0.5)
    return result.astype(jnp.bfloat16)


def draw_video(key, part):
    sample = jax.random.normal(jax.random.fold_in(key, 701), (VIDEOS, LMAX, D), jnp.float32)
    sample = jnp.clip(sample, -6.0, 6.0)
    return sample.astype(jnp.bfloat16)


def set_ends(drawn, stream_key, smallest, largest):
    longest = drawn.shape.index(max(drawn.shape))
    spots = []
    for shift in (0, 1):
        where = [jax.random.randint(jax.random.fold_in(stream_key, axis), (), 0, length) for axis, length in enumerate(drawn.shape)]
        where[longest] = (where[longest] + shift) % drawn.shape[longest]
        spots.append(tuple(where))
    return drawn.at[spots[0]].set(smallest).at[spots[1]].set(largest)


def block_levels(key, shape, cuts, smallest, largest):
    level = 1.0
    for dim, shards_of in cuts:
        heights = jax.random.uniform(jax.random.fold_in(jax.random.fold_in(key, 6), dim), (shards_of,), jnp.float32, smallest / len(cuts), largest / len(cuts))
        level = level * jnp.repeat(jnp.exp(heights), shape[dim] // shards_of).reshape((-1,) + (1,) * (len(shape) - 1 - dim))
    return level


def centred(own_key, extent, deviation, bound, split=(), kind=jnp.bfloat16):
    values = jax.random.normal(own_key, extent, jnp.float32) * deviation
    if len(split) > 0:
        values = block_levels(own_key, extent, split, -0.22, 0.18) * values
    return jnp.clip(values, min=-bound, max=bound).astype(kind)


def setup_inputs(seed: int = 0) -> dict:
    keys = jax.random.split(jax.random.key(seed), 18)
    video = draw_video(jax.random.fold_in(keys[17], 71), 0)
    video_length = set_ends(jax.random.randint(keys[1], (VIDEOS,), LMAX // 4, LMAX + 1), jax.random.fold_in(keys[1], 1), LMAX // 4, LMAX).astype(jnp.int32)
    prompt = centred(keys[2], (PROMPTS, PLEN, DT), 1.0, 6.0, ((0, 16), (1, 16)))
    prompt_length = set_ends(jax.random.randint(keys[3], (PROMPTS,), PLEN // 4, PLEN + 1), jax.random.fold_in(keys[3], 1), PLEN // 4, PLEN).astype(jnp.int32)
    prompt_choice = set_ends(jax.random.randint(keys[4], (VIDEOS,), 0, PROMPTS), jax.random.fold_in(keys[4], 1), 0, PROMPTS - 1).astype(jnp.int32)
    ffn_gain = jnp.clip(1.0 + 0.18 * jax.random.normal(keys[5], (DT,), jnp.float32), 0.1, 1.9)
    ffn_gate = centred(keys[6], (DT, FFT), DT ** -0.5, 0.09375, ((1, 16),))
    ffn_up = centred(keys[7], (DT, FFT), DT ** -0.5, 0.09375, ((1, 16),))
    ffn_down = centred(keys[8], (FFT, DT), FFT ** -0.5, 0.078125, ((0, 16),))
    final_gain = jnp.clip(1.0 + 0.18 * jax.random.normal(keys[9], (DT,), jnp.float32), 0.1, 1.9)
    video_gain = jnp.clip(1.0 + 0.18 * jax.random.normal(keys[10], (D,), jnp.float32), 0.1, 1.9)
    w_query = draw_w_query(jax.random.fold_in(keys[17], 71), 0)
    w_key = draw_w_key(jax.random.fold_in(keys[17], 71), 0)
    w_value = centred(keys[13], (D, D), D ** -0.5, 0.09375, ((0, 16), (1, 16)))
    w_text_key = centred(keys[14], (DT, D), DT ** -0.5, 0.09375, ((0, 16), (1, 16)))
    w_text_value = centred(keys[15], (DT, D), DT ** -0.5, 0.09375, ((0, 16), (1, 16)))
    w_out = centred(keys[16], (D, D), D ** -0.5, 0.09375, ((0, 16), (1, 16)))
    return dict(video=video, video_length=video_length, prompt=prompt, prompt_length=prompt_length, prompt_choice=prompt_choice, ffn_gain=ffn_gain, ffn_gate=ffn_gate, ffn_up=ffn_up, ffn_down=ffn_down, final_gain=final_gain, video_gain=video_gain, w_query=w_query, w_key=w_key, w_value=w_value, w_text_key=w_text_key, w_text_value=w_text_value, w_out=w_out)


epsilon = 1e-06

def rms_norm(values, gain):
    return values * lax.rsqrt(lax.optimization_barrier(jnp.mean(values * values, axis=-1, keepdims=True)) + epsilon) * gain

def reference(video, video_length, prompt, prompt_length, prompt_choice, ffn_gain, ffn_gate, ffn_up, ffn_down, final_gain, video_gain, w_query, w_key, w_value, w_text_key, w_text_value, w_out):

    def encode_one(prompt_rows):
        residual = prompt_rows.astype(jnp.float32)
        ffn_normed = rms_norm(residual, ffn_gain).astype(jnp.bfloat16)
        gate_proj = jnp.dot(ffn_normed, ffn_gate, preferred_element_type=jnp.float32)
        up_proj = jnp.dot(ffn_normed, ffn_up, preferred_element_type=jnp.float32)
        ffn_hidden = (jax.nn.gelu(gate_proj, approximate=True) * up_proj).astype(jnp.bfloat16)
        encoded = residual + jnp.dot(ffn_hidden, ffn_down, preferred_element_type=jnp.float32)
        text = rms_norm(encoded, final_gain).astype(jnp.bfloat16)
        text_key = jnp.dot(text, w_text_key, preferred_element_type=jnp.float32).astype(jnp.bfloat16)
        text_value = jnp.dot(text, w_text_value, preferred_element_type=jnp.float32).astype(jnp.bfloat16)
        return (text_key, text_value)
    all_text_keys, all_text_values = lax.map(encode_one, prompt)
    score_scale = HD ** (-0.5)

    def attend_one(packed):
        frames, frame_length, prompt_pick = packed
        residual = frames.astype(jnp.float32)
        normed = rms_norm(residual, video_gain).astype(jnp.bfloat16)
        query = jnp.dot(normed, w_query, preferred_element_type=jnp.float32).astype(jnp.bfloat16)
        key_rows = jnp.dot(normed, w_key, preferred_element_type=jnp.float32).astype(jnp.bfloat16)
        value_rows = jnp.dot(normed, w_value, preferred_element_type=jnp.float32).astype(jnp.bfloat16)
        text_key = lax.dynamic_index_in_dim(all_text_keys, prompt_pick, 0, keepdims=False)
        text_value = lax.dynamic_index_in_dim(all_text_values, prompt_pick, 0, keepdims=False)
        text_live = lax.dynamic_index_in_dim(prompt_length, prompt_pick, 0, keepdims=False)
        joint_keys = jnp.concatenate([key_rows, text_key], axis=0).astype(jnp.float32).reshape(LMAX + PLEN, HEADS, HD)
        joint_values = jnp.concatenate([value_rows, text_value], axis=0).astype(jnp.float32).reshape(LMAX + PLEN, HEADS, HD)
        query_heads = query.astype(jnp.float32).reshape(LMAX, HEADS, HD)
        scores = jnp.einsum('qhd,khd->hqk', query_heads, joint_keys) * score_scale
        position = jnp.arange(LMAX + PLEN, dtype=jnp.int32)
        live_keys = jnp.where(position < LMAX, position < frame_length, position - LMAX < text_live)
        scores = jnp.where(live_keys[None, None, :], scores, -1e+30)
        probs = jax.nn.softmax(scores, axis=-1).astype(jnp.bfloat16)
        attended = jnp.einsum('hqk,khd->qhd', probs.astype(jnp.float32), joint_values)
        attended = attended.astype(jnp.bfloat16).reshape(LMAX, HEADS * HD)
        projected = jnp.dot(attended, w_out, preferred_element_type=jnp.float32)
        row_live = jnp.arange(LMAX, dtype=jnp.int32) < frame_length
        return (residual + jnp.where(row_live[:, None], projected, 0.0)).astype(jnp.bfloat16)
    return lax.map(attend_one, (video, video_length, prompt_choice))
```

```python
import jax
import jax.numpy as jnp
from jax import lax
from jax.experimental import pallas as pl
from jax.experimental.pallas import tpu as pltpu
from jax.sharding import PartitionSpec as P

HD = 128
EPSILON = 1e-06
MESH = pl.DeviceIdType.MESH
BF = jnp.bfloat16
F32 = jnp.float32

TK, TV, Q, K, V, O, PROMPT = range(7)


def rms_norm(values, gain):
    return values * lax.rsqrt(jnp.mean(values * values, axis=-1, keepdims=True) + EPSILON) * gain


def kernel(
    length_ref,
    prompt_length_ref,
    choice_ref,
    video_ref,
    prompt_ref,
    ffn_gain_ref,
    final_gain_ref,
    video_gain_ref,
    gate_hbm,
    up_hbm,
    down_hbm,
    w_text_key,
    w_text_value,
    w_query,
    w_key,
    w_value,
    w_out,
    out_ref,
    W,
    PB,
    SEL,
    PG,
    FN,
    gate_ref,
    up_ref,
    down_ref,
    gate_acc,
    up_acc,
    hidden,
    FP,
    FR,
    TX,
    TG,
    NV,
    XG,
    q_acc,
    k_acc,
    v_acc,
    queries,
    keys,
    values,
    SB,
    RR,
    info_own,
    info,
    ffn_sem,
    ring_recv,
    ring_send,
    swap_send,
    sib_recv,
    info_sem,
    group_recv,
    group_send,
    group_send0,
):
    vid, seq = lax.axis_index("vid"), lax.axis_index("seq")
    yh, z = vid // 8, vid % 8
    x, yl, c = seq // 4, (seq // 2) % 2, seq % 2
    y = yh * 2 + yl
    diag = c == yh
    head_block = x * 4 + yl * 2 + yh

    partner = ((1 - yh) * 8 + z, seq + 1 - 2 * c)
    sibling = (vid, seq + 1 - 2 * c)
    z_right = (yh * 8 + (z + 1) % 8, seq)
    z_left = (yh * 8 + (z + 7) % 8, seq)

    def to_chip(k):
        xk, yk = (x + k // 4) % 4, (y + k % 4) % 4
        return ((yk // 2) * 8 + z, xk * 4 + (yk % 2) * 2 + yh)

    def place(k):
        return ((x + k // 4) % 4) * 4 + ((yl + (k // 2) % 2) % 2) * 2 + (c + k % 2) % 2

    def local(src, dst, sem):
        return pltpu.make_async_copy(src, dst, sem)

    def remote(src, dst, send, recv, device):
        return pltpu.make_async_remote_copy(
            src_ref=src, dst_ref=dst, send_sem=send, recv_sem=recv, device_id=device, device_id_type=MESH
        )

    ffn_copies = [
        local(gate_hbm, gate_ref, ffn_sem.at[0]),
        local(up_hbm, up_ref, ffn_sem.at[1]),
        local(down_hbm, down_ref, ffn_sem.at[2]),
    ]
    for copy in ffn_copies:
        copy.start()

    barrier = pltpu.get_barrier_semaphore()

    def greet(k, carry):
        seq_k = (seq + k) % 16
        vid_k = ((yh + k // 16) % 2) * 8 + z
        pl.semaphore_signal(barrier, inc=1, device_id=(vid_k, seq_k), device_id_type=MESH)
        return carry

    lax.fori_loop(1, 32, greet, 0)
    for neighbour in (z_left, z_right):
        pl.semaphore_signal(barrier, inc=1, device_id=neighbour, device_id_type=MESH)

    choice = choice_ref[0]
    row = lax.broadcasted_iota(jnp.int32, (8, 128), 0)
    text_live = prompt_length_ref[choice]
    info_own[...] = jnp.where(row == 0, choice, jnp.where(row == 1, length_ref[0], text_live))

    pl.semaphore_wait(barrier, 33)

    sources = [w_text_key, w_text_value, w_query, w_key, w_value, w_out, prompt_ref.at[0]]

    def slot(w, block):
        return PB.at[block] if w == PROMPT else W.at[w, block]

    def swap_copy(w):
        return remote(
            sources[w], slot(w, (1 - c) * 8 + z), swap_send.at[w], ring_recv.at[w, z], partner
        )

    def swap_local(w):
        return local(sources[w], slot(w, c * 8 + z), ring_recv.at[w, z])

    info_copy = remote(info_own, info, swap_send.at[7], info_sem, partner)
    info_local = local(info_own, info, info_sem)

    @pl.when(diag)
    def _():
        swap_local(PROMPT).start()
        info_local.start()
        for w in range(6):
            swap_local(w).start()

    @pl.when(jnp.logical_not(diag))
    def _():
        swap_copy(PROMPT).start()
        info_copy.start()
        for w in range(6):
            swap_copy(w).start()

    def ring_wait(w, zz):
        ref = slot(w, c * 8 + zz)
        local(ref, ref, ring_recv.at[w, zz]).wait()

    def ring_to(w, zz, device):
        ref = slot(w, c * 8 + zz)
        remote(ref, ref, ring_send.at[w], ring_recv.at[w, zz], device).start()

    def to_sibling(w, zz):
        ref = slot(w, c * 8 + zz)
        remote(ref, ref, ring_send.at[w], sib_recv.at[w], sibling).start()

    def own(w):
        ring_wait(w, z)
        ring_to(w, z, z_right)
        ring_to(w, z, z_left)
        to_sibling(w, z)

    def hop(w, k):
        right_hops = 4 if w % 2 == 0 else 3
        left_hops = 7 - right_hops
        from_left, from_right = (z + 8 - k) % 8, (z + k) % 8
        if k <= right_hops:
            ring_wait(w, from_left)
            if k < right_hops:
                ring_to(w, from_left, z_right)
        if k <= left_hops:
            ring_wait(w, from_right)
            if k < left_hops:
                ring_to(w, from_right, z_left)
        if k <= right_hops:
            to_sibling(w, from_left)
        if k <= left_hops:
            to_sibling(w, from_right)

    def sibling_wait(w):
        ref = PB.at[pl.ds(0, 8)] if w == PROMPT else W.at[w, pl.ds(0, 8)]
        local(ref, ref, sib_recv.at[w]).wait()

    own(PROMPT)
    own(TK)
    own(TV)

    NV[...] = rms_norm(video_ref[0].astype(F32), video_gain_ref[...]).astype(BF)

    for k in range(1, 5):
        hop(PROMPT, k)
    hop(TK, 1)
    hop(TV, 1)

    sibling_wait(PROMPT)
    local(info, info, info_sem).wait()
    wanted = info[0:1, 0:1]

    def pick(i, total):
        return total + jnp.where(wanted == i, PB[i].astype(F32), 0.0)

    SEL[...] = lax.fori_loop(0, 16, pick, jnp.zeros(SEL.shape, F32)).astype(BF)

    PROMPTS, SUMS, TEXT, VIDEO, OUT = range(5)

    def send_prompt(k):
        return remote(
            SEL, PG.at[head_block], group_send.at[PROMPTS], group_recv.at[PROMPTS], (c * 8 + z, place(k))
        )

    def spread(first, last, make):
        def step(k, carry):
            make(k).start()
            return carry

        lax.fori_loop(first, last, step, 0)

    def first_send(copy, copy_local, group):
        @pl.when(diag)
        def _():
            copy_local.start()

        @pl.when(jnp.logical_not(diag))
        def _():
            copy.start()

    prompt0 = remote(
        SEL, PG.at[head_block], group_send0.at[PROMPTS], group_recv.at[PROMPTS], (c * 8 + z, seq)
    )
    first_send(prompt0, local(SEL, PG.at[head_block], group_recv.at[PROMPTS]), PROMPTS)
    spread(1, 16, send_prompt)

    def send_video(k):
        return remote(NV, XG.at[seq], group_send.at[VIDEO], group_recv.at[VIDEO], to_chip(k))

    video0 = remote(NV, XG.at[seq], group_send0.at[VIDEO], group_recv.at[VIDEO], to_chip(0))
    first_send(video0, local(NV, XG.at[seq], group_recv.at[VIDEO]), VIDEO)
    spread(1, 16, send_video)

    hop(TK, 2)
    hop(TV, 2)
    own(Q)
    own(K)

    local(PG, PG, group_recv.at[PROMPTS]).wait()

    def norm_rows(i, carry):
        rows = PG[pl.ds(2 * i, 2)].astype(F32).reshape(16, PG.shape[2])
        FN[pl.ds(pl.multiple_of(i * 16, 16), 16), :] = rms_norm(rows, ffn_gain_ref[...]).astype(BF)
        return carry

    lax.fori_loop(0, 8, norm_rows, 0)
    ffn_copies[0].wait()
    ffn_copies[1].wait()
    gate_acc[...] = jnp.zeros_like(gate_acc)
    up_acc[...] = jnp.zeros_like(up_acc)

    def gate_up(i, carry):
        at = pl.ds(pl.multiple_of(i * 512, 512), 512)
        rows = FN[:, at]
        gate_acc[...] += jnp.dot(rows, gate_ref[at, :], preferred_element_type=F32)
        up_acc[...] += jnp.dot(rows, up_ref[at, :], preferred_element_type=F32)
        return carry

    lax.fori_loop(0, 8, gate_up, 0)
    hidden[...] = (jax.nn.gelu(gate_acc[...], approximate=True) * up_acc[...]).astype(BF)

    hop(TK, 3)
    hop(TV, 3)
    hop(Q, 1)
    hop(K, 1)
    ffn_copies[2].wait()

    def down_proj(i, carry):
        at = pl.ds(pl.multiple_of(i * 256, 256), 256)
        part = jnp.dot(hidden[...], down_ref[:, at], preferred_element_type=F32)
        FP[:, :, at] = part.reshape(16, 8, 256).astype(BF)
        return carry

    lax.fori_loop(0, 16, down_proj, 0)

    def send_sums(k):
        return remote(
            FP.at[place(k)], FR.at[seq], group_send.at[SUMS], group_recv.at[SUMS], (vid, place(k))
        )

    local(FP.at[seq], FR.at[seq], group_recv.at[SUMS]).start()
    spread(1, 16, send_sums)

    hop(TK, 4)
    hop(TV, 4)
    hop(Q, 2)
    hop(K, 2)
    own(V)
    own(O)

    local(FR, FR, group_recv.at[SUMS]).wait()
    encoded = lax.fori_loop(
        0, 16, lambda i, total: total + FR[i].astype(F32), jnp.zeros(TX.shape, F32)
    )
    encoded = PG[seq].astype(F32) + encoded
    TX[...] = rms_norm(encoded, final_gain_ref[...]).astype(BF)

    def send_text(k):
        return remote(TX, TG.at[seq], group_send.at[TEXT], group_recv.at[TEXT], to_chip(k))

    text0 = remote(TX, TG.at[seq], group_send0.at[TEXT], group_recv.at[TEXT], to_chip(0))
    first_send(text0, local(TX, TG.at[seq], group_recv.at[TEXT]), TEXT)
    spread(1, 16, send_text)

    hop(Q, 3)
    hop(K, 3)
    hop(V, 1)
    hop(O, 1)
    hop(Q, 4)
    hop(K, 4)
    hop(V, 2)
    hop(O, 2)

    local(XG, XG, group_recv.at[VIDEO]).wait()
    sibling_wait(Q)
    sibling_wait(K)
    q_acc[...] = jnp.zeros_like(q_acc)
    k_acc[...] = jnp.zeros_like(k_acc)

    def video_rows(j):
        at = pl.ds(pl.multiple_of(j * 256, 256), 256)
        return XG[:, :, at].reshape(512, 256)

    def query_key(j, carry):
        rows = video_rows(j)
        q_acc[...] += jnp.dot(rows, W[Q, j], preferred_element_type=F32)
        k_acc[...] += jnp.dot(rows, W[K, j], preferred_element_type=F32)
        return carry

    lax.fori_loop(0, 16, query_key, 0)
    queries[...] = q_acc[...].astype(BF)
    keys[pl.ds(0, 512), :] = k_acc[...].astype(BF)

    hop(V, 3)
    hop(O, 3)

    local(TG, TG, group_recv.at[TEXT]).wait()
    sibling_wait(TK)
    sibling_wait(TV)

    def text_key_value(j, carry):
        at = pl.ds(pl.multiple_of(j * 256, 256), 256)
        rows = TG[:, :, at].astype(F32).reshape(128, 256).astype(BF)
        key_sum, value_sum = carry
        key_sum = key_sum + jnp.dot(rows, W[TK, j], preferred_element_type=F32)
        value_sum = value_sum + jnp.dot(rows, W[TV, j], preferred_element_type=F32)
        return key_sum, value_sum

    zero = jnp.zeros((128, 256), F32)
    text_key, text_value = lax.fori_loop(0, 16, text_key_value, (zero, zero))
    keys[pl.ds(512, 128), :] = text_key.astype(BF)
    values[pl.ds(512, 128), :] = text_value.astype(BF)

    hop(V, 4)
    hop(O, 4)
    sibling_wait(V)
    v_acc[...] = jnp.zeros_like(v_acc)

    def value_rows(j, carry):
        v_acc[...] += jnp.dot(video_rows(j), W[V, j], preferred_element_type=F32)
        return carry

    lax.fori_loop(0, 16, value_rows, 0)
    values[pl.ds(0, 512), :] = v_acc[...].astype(BF)
    sibling_wait(O)

    position = lax.broadcasted_iota(jnp.int32, (1, 640), 1)
    live = position < jnp.where(position < 512, info[1:2, 0:1], info[2:3, 0:1] + 512)

    def send_out(block):
        return remote(
            SB.at[block], RR.at[head_block], group_send.at[OUT], group_recv.at[OUT], (c * 8 + z, block)
        )

    out0_local = local(SB.at[seq], RR.at[head_block], group_recv.at[OUT])
    out0 = remote(
        SB.at[seq], RR.at[head_block], group_send0.at[OUT], group_recv.at[OUT], (c * 8 + z, seq)
    )

    def attend(i, carry):
        part = (x + i) % 4
        rows = pl.ds(pl.multiple_of(part * 128, 128), 128)
        heads = []
        for h in range(2):
            lanes = pl.ds(h * HD, HD)
            scores = lax.dot_general(
                queries[rows, lanes], keys[:, lanes], (((1,), (1,)), ((), ())), preferred_element_type=F32
            )
            scores = jnp.where(live, scores * HD ** (-0.5), -1e30)
            e = jnp.exp(scores - jnp.max(scores, axis=-1, keepdims=True))
            probs = (e / jnp.sum(e, axis=-1, keepdims=True)).astype(BF)
            heads.append(jnp.dot(probs, values[:, lanes], preferred_element_type=F32).astype(BF))
        attended = jnp.concatenate(heads, axis=1)

        for j in range(16):
            projected = jnp.dot(attended, W[O, j], preferred_element_type=F32)
            SB[pl.ds(part * 4, 4), :, pl.ds(j * 256, 256)] = projected.reshape(4, 32, 256).astype(BF)

        def send(k, carry):
            block = part * 4 + (seq + k) % 4

            @pl.when(block != seq)
            def _():
                send_out(block).start()

            @pl.when(block == seq)
            def _():
                first_send(out0, out0_local, OUT)

            return carry

        lax.fori_loop(0, 4, send, 0)
        return carry

    lax.fori_loop(0, 4, attend, 0)

    local(RR, RR, group_recv.at[OUT]).wait()
    row_position = seq * 32 + lax.broadcasted_iota(jnp.int32, (32, 1), 0)
    row_live = row_position < length_ref[0]

    def add_up(j, carry):
        at = pl.ds(pl.multiple_of(j * 512, 512), 512)
        total = RR[0, :, at].astype(F32)
        for i in range(1, 16):
            total = total + RR[i, :, at].astype(F32)
        updated = video_ref[0, :, at].astype(F32) + jnp.where(row_live, total, 0.0)
        out_ref[0, :, at] = updated.astype(BF)
        return carry

    lax.fori_loop(0, 8, add_up, 0)

    @pl.when(jnp.logical_not(diag))
    def _():
        for w in range(7):
            swap_copy(w).wait_send()
        info_copy.wait_send()
        for group, copy in ((PROMPTS, prompt0), (TEXT, text0), (VIDEO, video0), (OUT, out0)):
            copy.wait_send()

    for w in range(7):
        ref = PB.at[pl.ds(0, 15)] if w == PROMPT else W.at[w, pl.ds(0, 15)]
        local(ref, ref, ring_send.at[w]).wait()
    for group, buffer in ((PROMPTS, PG), (SUMS, FR), (TEXT, TG), (VIDEO, XG), (OUT, RR)):
        ref = buffer.at[pl.ds(0, 15)]
        local(ref, ref, group_send.at[group]).wait()


def block(
    video,
    video_length,
    prompt,
    prompt_length,
    prompt_choice,
    ffn_gain,
    ffn_gate,
    ffn_up,
    ffn_down,
    final_gain,
    video_gain,
    w_query,
    w_key,
    w_value,
    w_text_key,
    w_text_value,
    w_out,
):
    smem = pl.BlockSpec(memory_space=pltpu.SMEM)
    vmem = pl.BlockSpec(memory_space=pltpu.VMEM)
    hbm = pl.BlockSpec(memory_space=pl.ANY)
    dma = pltpu.SemaphoreType.DMA
    width = 4096
    return pl.pallas_call(
        kernel,
        out_shape=jax.ShapeDtypeStruct(video.shape, video.dtype),
        in_specs=[smem] * 3 + [vmem] * 5 + [hbm] * 9,
        out_specs=vmem,
        scratch_shapes=[
            pltpu.VMEM((6, 16, 256, 256), BF),
            pltpu.VMEM((16, 8, width), BF),
            pltpu.VMEM((8, width), BF),
            pltpu.VMEM((16, 8, width), BF),
            pltpu.VMEM((128, width), BF),
            pltpu.VMEM(ffn_gate.shape, BF),
            pltpu.VMEM(ffn_up.shape, BF),
            pltpu.VMEM(ffn_down.shape, BF),
            pltpu.VMEM((128, 384), F32),
            pltpu.VMEM((128, 384), F32),
            pltpu.VMEM((128, 384), BF),
            pltpu.VMEM((16, 8, width), BF),
            pltpu.VMEM((16, 8, width), BF),
            pltpu.VMEM((8, width), BF),
            pltpu.VMEM((16, 8, width), BF),
            pltpu.VMEM((32, width), BF),
            pltpu.VMEM((16, 32, width), BF),
            pltpu.VMEM((512, 256), F32),
            pltpu.VMEM((512, 256), F32),
            pltpu.VMEM((512, 256), F32),
            pltpu.VMEM((512, 256), BF),
            pltpu.VMEM((640, 256), BF),
            pltpu.VMEM((640, 256), BF),
            pltpu.VMEM((16, 32, width), BF),
            pltpu.VMEM((16, 32, width), BF),
            pltpu.VMEM((8, 128), jnp.int32),
            pltpu.VMEM((8, 128), jnp.int32),
            dma((3,)),
            dma((7, 8)),
            dma((7,)),
            dma((8,)),
            dma((7,)),
            dma,
            dma((5,)),
            dma((5,)),
            dma((5,)),
        ],
        compiler_params=pltpu.CompilerParams(
            collective_id=0, has_side_effects=True, vmem_limit_bytes=58 * 1024 * 1024
        ),
        name="joint_attention",
    )(
        video_length,
        prompt_length,
        prompt_choice,
        video,
        prompt,
        ffn_gain.reshape(1, -1),
        final_gain.reshape(1, -1),
        video_gain.reshape(1, -1),
        ffn_gate,
        ffn_up,
        ffn_down,
        w_text_key,
        w_text_value,
        w_query,
        w_key,
        w_value,
        w_out,
    )


def solution(mesh):
    in_specs = (
        P("vid", "seq", None),
        P("vid"),
        P("vid", "seq", None),
        P(),
        P("vid"),
        P(),
        P(None, "seq"),
        P(None, "seq"),
        P("seq", None),
        P(),
        P(),
        P("vid", "seq"),
        P("vid", "seq"),
        P("vid", "seq"),
        P("vid", "seq"),
        P("vid", "seq"),
        P("seq", "vid"),
    )
    out_specs = P("vid", "seq", None)
    return jax.shard_map(block, mesh=mesh, in_specs=in_specs, out_specs=out_specs, check_vma=False)
```

```python
import jax
import jax.numpy as jnp
from jax import lax
from jax.experimental import pallas as pl
from jax.experimental.pallas import tpu as pltpu
from jax.sharding import PartitionSpec as P

HD = 128
EPSILON = 1e-06
MESH = pl.DeviceIdType.MESH
BF = jnp.bfloat16
F32 = jnp.float32

TK, TV, Q, K, V, O, PROMPT = range(7)


def rms_norm(values, gain):
    return values * lax.rsqrt(jnp.mean(values * values, axis=-1, keepdims=True) + EPSILON) * gain


def kernel(
    length_ref,
    prompt_length_ref,
    choice_ref,
    video_ref,
    prompt_ref,
    ffn_gain_ref,
    final_gain_ref,
    video_gain_ref,
    gate_hbm,
    up_hbm,
    down_hbm,
    w_text_key,
    w_text_value,
    w_query,
    w_key,
    w_value,
    w_out,
    out_ref,
    W,
    PB,
    SEL,
    PG,
    FN,
    gate_ref,
    up_ref,
    down_ref,
    gate_acc,
    up_acc,
    hidden,
    FP,
    FR,
    TX,
    TG,
    NV,
    XG,
    q_acc,
    k_acc,
    v_acc,
    queries,
    keys,
    values,
    SB,
    XR,
    YR,
    XS,
    YS,
    RR,
    info_own,
    info,
    ffn_sem,
    ring_recv,
    ring_send,
    swap_send,
    sib_recv,
    info_sem,
    group_recv,
    group_send,
    group_send0,
    video_recv,
    video_send,
    out_recv,
    out_send,
):
    vid, seq = lax.axis_index("vid"), lax.axis_index("seq")
    yh, z = vid // 8, vid % 8
    x, yl, c = seq // 4, (seq // 2) % 2, seq % 2
    y = yh * 2 + yl
    diag = c == yh
    head_block = x * 4 + yl * 2 + yh

    partner = ((1 - yh) * 8 + z, seq + 1 - 2 * c)
    sibling = (vid, seq + 1 - 2 * c)
    z_right = (yh * 8 + (z + 1) % 8, seq)
    z_left = (yh * 8 + (z + 7) % 8, seq)

    def to_chip(k):
        xk, yk = (x + k // 4) % 4, (y + k % 4) % 4
        return ((yk // 2) * 8 + z, xk * 4 + (yk % 2) * 2 + yh)

    def place(k):
        return ((x + k // 4) % 4) * 4 + ((yl + (k // 2) % 2) % 2) * 2 + (c + k % 2) % 2

    def local(src, dst, sem):
        return pltpu.make_async_copy(src, dst, sem)

    def remote(src, dst, send, recv, device):
        return pltpu.make_async_remote_copy(
            src_ref=src, dst_ref=dst, send_sem=send, recv_sem=recv, device_id=device, device_id_type=MESH
        )

    ffn_copies = [
        local(gate_hbm, gate_ref, ffn_sem.at[0]),
        local(up_hbm, up_ref, ffn_sem.at[1]),
        local(down_hbm, down_ref, ffn_sem.at[2]),
    ]
    for copy in ffn_copies:
        copy.start()

    barrier = pltpu.get_barrier_semaphore()

    def greet(k, carry):
        seq_k = (seq + k) % 16
        vid_k = ((yh + k // 16) % 2) * 8 + z
        pl.semaphore_signal(barrier, inc=1, device_id=(vid_k, seq_k), device_id_type=MESH)
        return carry

    lax.fori_loop(1, 32, greet, 0)
    for neighbour in (z_left, z_right):
        pl.semaphore_signal(barrier, inc=1, device_id=neighbour, device_id_type=MESH)

    choice = choice_ref[0]
    row = lax.broadcasted_iota(jnp.int32, (8, 128), 0)
    text_live = prompt_length_ref[choice]
    info_own[...] = jnp.where(row == 0, choice, jnp.where(row == 1, length_ref[0], text_live))

    normed = rms_norm(video_ref[0].astype(F32), video_gain_ref[...]).astype(BF)
    NV[0] = normed[:, :2048]
    NV[1] = normed[:, 2048:]

    pl.semaphore_wait(barrier, 33)

    sources = [w_text_key, w_text_value, w_query, w_key, w_value, w_out, prompt_ref.at[0]]

    def slot(w, block):
        return PB.at[block] if w == PROMPT else W.at[w, block]

    def swap_copy(w):
        return remote(
            sources[w], slot(w, (1 - c) * 8 + z), swap_send.at[w], ring_recv.at[w, z], partner
        )

    def swap_local(w):
        return local(sources[w], slot(w, c * 8 + z), ring_recv.at[w, z])

    info_copy = remote(info_own, info, swap_send.at[7], info_sem, partner)
    info_local = local(info_own, info, info_sem)

    @pl.when(diag)
    def _():
        swap_local(PROMPT).start()
        info_local.start()
        for w in range(6):
            swap_local(w).start()

    @pl.when(jnp.logical_not(diag))
    def _():
        swap_copy(PROMPT).start()
        info_copy.start()
        for w in range(6):
            swap_copy(w).start()

    def ring_wait(w, zz):
        ref = slot(w, c * 8 + zz)
        local(ref, ref, ring_recv.at[w, zz]).wait()

    def ring_to(w, zz, device):
        ref = slot(w, c * 8 + zz)
        remote(ref, ref, ring_send.at[w], ring_recv.at[w, zz], device).start()

    def to_sibling(w, zz):
        ref = slot(w, c * 8 + zz)
        remote(ref, ref, ring_send.at[w], sib_recv.at[w], sibling).start()

    def own(w):
        ring_wait(w, z)
        ring_to(w, z, z_right)
        ring_to(w, z, z_left)
        to_sibling(w, z)

    def hop(w, k):
        right_hops = 4 if w % 2 == 0 else 3
        left_hops = 7 - right_hops
        from_left, from_right = (z + 8 - k) % 8, (z + k) % 8
        if k <= right_hops:
            ring_wait(w, from_left)
            if k < right_hops:
                ring_to(w, from_left, z_right)
        if k <= left_hops:
            ring_wait(w, from_right)
            if k < left_hops:
                ring_to(w, from_right, z_left)
        if k <= right_hops:
            to_sibling(w, from_left)
        if k <= left_hops:
            to_sibling(w, from_right)

    def sibling_wait(w):
        ref = PB.at[pl.ds(0, 8)] if w == PROMPT else W.at[w, pl.ds(0, 8)]
        local(ref, ref, sib_recv.at[w]).wait()

    not_diag = jnp.logical_not(diag)

    def at_core(xk, yk, core):
        return ((yk // 2) * 8 + z, xk * 4 + (yk % 2) * 2 + core)

    def video_x(k):
        return remote(
            NV.at[0], XG.at[0, seq], video_send.at[0], video_recv.at[0], at_core((x + k) % 4, y, yh)
        )

    def video_y(k):
        return remote(
            NV.at[1], XG.at[1, seq], video_send.at[1], video_recv.at[1], at_core(x, (y + k) % 4, yh)
        )

    own_chip = [
        remote(
            NV.at[h], XG.at[h, seq], video_send.at[4], video_recv.at[h], sibling
        )
        for h in range(2)
    ]

    @pl.when(diag)
    def _():
        for h in range(2):
            local(NV.at[h], XG.at[h, seq], video_recv.at[h]).start()

    @pl.when(not_diag)
    def _():
        for h in range(2):
            own_chip[h].start()

    for k in (2, 1, 3):
        video_x(k).start()
        video_y(k).start()

    def lower_piece(i):
        return (i // 2) * 4 + yl * 2 + i % 2

    def lower_on(i, k):
        ref = XG.at[0, lower_piece(i)]
        return remote(ref, ref, video_send.at[2], video_recv.at[2], at_core(x, (y + k) % 4, c))

    def upper_on(k):
        ref = XG.at[1, pl.ds(x * 4, 4)]
        return remote(ref, ref, video_send.at[3], video_recv.at[3], at_core((x + k) % 4, y, c))

    def pass_video_on():
        ref = XG.at[1, pl.ds(0, 4)]
        local(ref, ref, video_recv.at[1]).wait()
        for k in (2, 1, 3):
            upper_on(k).start()

        @pl.when(diag)
        def _():
            ref = XG.at[0, pl.ds(0, 8)]
            local(ref, ref, video_recv.at[0]).wait()

            def step(i, carry):
                for k in (2, 1, 3):
                    lower_on(i, k).start()
                return carry

            lax.fori_loop(0, 8, step, 0)

    def video_wait():
        ref = XG.at[1, pl.ds(0, 12)]
        local(ref, ref, video_recv.at[3]).wait()

        @pl.when(diag)
        def _():
            ref = XG.at[0, pl.ds(0, 8)]
            local(ref, ref, video_recv.at[2]).wait()

        @pl.when(not_diag)
        def _():
            ref = XG.at[0]
            local(ref, ref, video_recv.at[2]).wait()

    own(PROMPT)
    own(TK)
    own(TV)

    for k in range(1, 5):
        hop(PROMPT, k)
    pass_video_on()
    hop(TK, 1)
    hop(TV, 1)

    sibling_wait(PROMPT)
    local(info, info, info_sem).wait()
    wanted = info[0:1, 0:1]

    def pick(i, total):
        return total + jnp.where(wanted == i, PB[i].astype(F32), 0.0)

    SEL[...] = lax.fori_loop(0, 16, pick, jnp.zeros(SEL.shape, F32)).astype(BF)

    PROMPTS, SUMS, TEXT = range(3)

    def send_prompt(k):
        return remote(
            SEL, PG.at[head_block], group_send.at[PROMPTS], group_recv.at[PROMPTS], (c * 8 + z, place(k))
        )

    def spread(first, last, make):
        def step(k, carry):
            make(k).start()
            return carry

        lax.fori_loop(first, last, step, 0)

    def first_send(copy, copy_local, group):
        @pl.when(diag)
        def _():
            copy_local.start()

        @pl.when(jnp.logical_not(diag))
        def _():
            copy.start()

    prompt0 = remote(
        SEL, PG.at[head_block], group_send0.at[PROMPTS], group_recv.at[PROMPTS], (c * 8 + z, seq)
    )
    first_send(prompt0, local(SEL, PG.at[head_block], group_recv.at[PROMPTS]), PROMPTS)
    spread(1, 16, send_prompt)

    hop(TK, 2)
    hop(TV, 2)
    own(Q)
    own(K)

    local(PG, PG, group_recv.at[PROMPTS]).wait()

    def norm_rows(i, carry):
        rows = PG[pl.ds(2 * i, 2)].astype(F32).reshape(16, PG.shape[2])
        FN[pl.ds(pl.multiple_of(i * 16, 16), 16), :] = rms_norm(rows, ffn_gain_ref[...]).astype(BF)
        return carry

    lax.fori_loop(0, 8, norm_rows, 0)
    ffn_copies[0].wait()
    ffn_copies[1].wait()
    gate_acc[...] = jnp.zeros_like(gate_acc)
    up_acc[...] = jnp.zeros_like(up_acc)

    def gate_up(i, carry):
        at = pl.ds(pl.multiple_of(i * 512, 512), 512)
        rows = FN[:, at]
        gate_acc[...] += jnp.dot(rows, gate_ref[at, :], preferred_element_type=F32)
        up_acc[...] += jnp.dot(rows, up_ref[at, :], preferred_element_type=F32)
        return carry

    lax.fori_loop(0, 8, gate_up, 0)
    hidden[...] = (jax.nn.gelu(gate_acc[...], approximate=True) * up_acc[...]).astype(BF)

    hop(TK, 3)
    hop(TV, 3)
    hop(Q, 1)
    hop(K, 1)
    ffn_copies[2].wait()

    def down_proj(i, carry):
        at = pl.ds(pl.multiple_of(i * 256, 256), 256)
        part = jnp.dot(hidden[...], down_ref[:, at], preferred_element_type=F32)
        FP[:, :, at] = part.reshape(16, 8, 256).astype(BF)
        return carry

    lax.fori_loop(0, 16, down_proj, 0)

    def send_sums(k):
        return remote(
            FP.at[place(k)], FR.at[seq], group_send.at[SUMS], group_recv.at[SUMS], (vid, place(k))
        )

    local(FP.at[seq], FR.at[seq], group_recv.at[SUMS]).start()
    spread(1, 16, send_sums)

    hop(TK, 4)
    hop(TV, 4)
    hop(Q, 2)
    hop(K, 2)
    own(V)
    own(O)

    local(FR, FR, group_recv.at[SUMS]).wait()
    encoded = lax.fori_loop(
        0, 16, lambda i, total: total + FR[i].astype(F32), jnp.zeros(TX.shape, F32)
    )
    encoded = PG[seq].astype(F32) + encoded
    TX[...] = rms_norm(encoded, final_gain_ref[...]).astype(BF)

    def send_text(k):
        return remote(TX, TG.at[seq], group_send.at[TEXT], group_recv.at[TEXT], to_chip(k))

    text0 = remote(TX, TG.at[seq], group_send0.at[TEXT], group_recv.at[TEXT], to_chip(0))
    first_send(text0, local(TX, TG.at[seq], group_recv.at[TEXT]), TEXT)
    spread(1, 16, send_text)

    hop(Q, 3)
    hop(K, 3)
    hop(V, 1)
    hop(O, 1)
    hop(Q, 4)
    hop(K, 4)
    hop(V, 2)
    hop(O, 2)

    video_wait()
    sibling_wait(Q)
    sibling_wait(K)
    q_acc[...] = jnp.zeros_like(q_acc)
    k_acc[...] = jnp.zeros_like(k_acc)

    def video_rows(j):
        at = pl.ds(pl.multiple_of((j % 8) * 256, 256), 256)
        return XG[j // 8, :, :, at].reshape(512, 256)

    def query_key(j, carry):
        rows = video_rows(j)
        q_acc[...] += jnp.dot(rows, W[Q, j], preferred_element_type=F32)
        k_acc[...] += jnp.dot(rows, W[K, j], preferred_element_type=F32)
        return carry

    lax.fori_loop(0, 16, query_key, 0)
    queries[...] = q_acc[...].astype(BF)
    keys[pl.ds(0, 512), :] = k_acc[...].astype(BF)

    hop(V, 3)
    hop(O, 3)

    local(TG, TG, group_recv.at[TEXT]).wait()
    sibling_wait(TK)
    sibling_wait(TV)

    def text_key_value(j, carry):
        at = pl.ds(pl.multiple_of(j * 256, 256), 256)
        rows = TG[:, :, at].astype(F32).reshape(128, 256).astype(BF)
        key_sum, value_sum = carry
        key_sum = key_sum + jnp.dot(rows, W[TK, j], preferred_element_type=F32)
        value_sum = value_sum + jnp.dot(rows, W[TV, j], preferred_element_type=F32)
        return key_sum, value_sum

    zero = jnp.zeros((128, 256), F32)
    text_key, text_value = lax.fori_loop(0, 16, text_key_value, (zero, zero))
    keys[pl.ds(512, 128), :] = text_key.astype(BF)
    values[pl.ds(512, 128), :] = text_value.astype(BF)

    hop(V, 4)
    hop(O, 4)
    sibling_wait(V)
    v_acc[...] = jnp.zeros_like(v_acc)

    def value_rows(j, carry):
        v_acc[...] += jnp.dot(video_rows(j), W[V, j], preferred_element_type=F32)
        return carry

    lax.fori_loop(0, 16, value_rows, 0)
    values[pl.ds(0, 512), :] = v_acc[...].astype(BF)
    sibling_wait(O)

    position = lax.broadcasted_iota(jnp.int32, (1, 640), 1)
    live = position < jnp.where(position < 512, info[1:2, 0:1], info[2:3, 0:1] + 512)

    def out_x(part):
        return remote(
            SB.at[0, pl.ds(part * 4, 4)],
            XR.at[(x + 3 - part) % 4],
            out_send.at[0],
            out_recv.at[0],
            at_core(part, y, c),
        )

    def out_y(part, k):
        return remote(
            SB.at[1, pl.ds(part * 4 + k * 2, 2)],
            YR.at[(y + 3 - (c * 2 + k)) % 4, pl.ds(part * 2, 2)],
            out_send.at[1 + k],
            out_recv.at[1],
            at_core(x, c * 2 + k, c),
        )

    def sum_x(k):
        return remote(
            XS.at[k], RR.at[0, y], out_send.at[3 + k], out_recv.at[2], at_core(x, c * 2 + k // 2, k % 2)
        )

    def sum_y(xk, core, send):
        return remote(
            YS.at[xk * 2 + core], RR.at[1, x], send, out_recv.at[3], at_core(xk, y, core)
        )

    def attend(i, carry):
        part = (x + 1 + i) % 4
        rows = pl.ds(pl.multiple_of(part * 128, 128), 128)
        heads = []
        for h in range(2):
            lanes = pl.ds(h * HD, HD)
            scores = lax.dot_general(
                queries[rows, lanes], keys[:, lanes], (((1,), (1,)), ((), ())), preferred_element_type=F32
            )
            scores = jnp.where(live, scores * HD ** (-0.5), -1e30)
            e = jnp.exp(scores - jnp.max(scores, axis=-1, keepdims=True))
            probs = (e / jnp.sum(e, axis=-1, keepdims=True)).astype(BF)
            heads.append(jnp.dot(probs, values[:, lanes], preferred_element_type=F32).astype(BF))
        attended = jnp.concatenate(heads, axis=1)

        for j in range(16):
            projected = jnp.dot(attended, W[O, j], preferred_element_type=F32)
            SB[j // 8, pl.ds(part * 4, 4), :, pl.ds((j % 8) * 256, 256)] = projected.reshape(4, 32, 256).astype(BF)

        @pl.when(part != x)
        def _():
            out_x(part).start()

        for k in range(2):

            @pl.when(y != c * 2 + k)
            def _():
                out_y(part, k).start()

        return carry

    lax.fori_loop(0, 4, attend, 0)

    local(XR, XR, out_recv.at[0]).wait()
    for k in range(4):
        for lanes in (pl.ds(0, 1024), pl.ds(1024, 1024)):
            total = SB[0, x * 4 + k, :, lanes].astype(F32)
            for i in range(3):
                total = total + XR[i, k, :, lanes].astype(F32)
            XS[k, :, lanes] = total.astype(BF)
        to_here = jnp.logical_and(diag, jnp.logical_and(yl == k // 2, c == k % 2))

        @pl.when(to_here)
        def _():
            local(XS.at[k], RR.at[0, y], out_recv.at[2]).start()

        @pl.when(jnp.logical_not(to_here))
        def _():
            sum_x(k).start()

    @pl.when(diag)
    def _():
        local(YR, YR, out_recv.at[1]).wait()

        def step(i, carry):
            xk, core = (x + 1 + i // 2) % 4, (c + 1 + i) % 2
            for lanes in (pl.ds(0, 1024), pl.ds(1024, 1024)):
                total = SB[1, xk * 4 + yl * 2 + core, :, lanes].astype(F32)
                for j in range(3):
                    total = total + YR[j, xk * 2 + core, :, lanes].astype(F32)
                YS[xk * 2 + core, :, lanes] = total.astype(BF)

            @pl.when(i < 7)
            def _():
                sum_y(xk, core, out_send.at[7]).start()

            @pl.when(i == 7)
            def _():
                local(YS.at[xk * 2 + core], RR.at[1, x], out_recv.at[3]).start()

            return carry

        lax.fori_loop(0, 8, step, 0)

    local(RR.at[0], RR.at[0], out_recv.at[2]).wait()
    local(RR.at[1], RR.at[1], out_recv.at[3]).wait()
    row_position = seq * 32 + lax.broadcasted_iota(jnp.int32, (32, 1), 0)
    row_live = row_position < length_ref[0]

    for half in range(2):
        for j in range(4):
            at = pl.ds(j * 512, 512)
            total = RR[half, 0, :, at].astype(F32)
            for i in range(1, 4):
                total = total + RR[half, i, :, at].astype(F32)
            at = pl.ds(half * 2048 + j * 512, 512)
            updated = video_ref[0, :, at].astype(F32) + jnp.where(row_live, total, 0.0)
            out_ref[0, :, at] = updated.astype(BF)

    @pl.when(jnp.logical_not(diag))
    def _():
        for w in range(7):
            swap_copy(w).wait_send()
        info_copy.wait_send()
        prompt0.wait_send()
        text0.wait_send()
        both = XG.at[0, pl.ds(0, 2)]
        local(both, both, video_send.at[4]).wait()

    for w in range(7):
        ref = PB.at[pl.ds(0, 15)] if w == PROMPT else W.at[w, pl.ds(0, 15)]
        local(ref, ref, ring_send.at[w]).wait()
    for group, buffer in ((PROMPTS, PG), (SUMS, FR), (TEXT, TG)):
        ref = buffer.at[pl.ds(0, 15)]
        local(ref, ref, group_send.at[group]).wait()
    for sem, pieces in ((video_send.at[0], 3), (video_send.at[1], 3), (video_send.at[3], 12), (out_send.at[0], 12)):
        ref = XG.at[0, pl.ds(0, pieces)]
        local(ref, ref, sem).wait()
    for k in range(2):

        @pl.when(y != c * 2 + k)
        def _():
            ref = XG.at[0, pl.ds(0, 8)]
            local(ref, ref, out_send.at[1 + k]).wait()

    for k in range(4):
        to_here = jnp.logical_and(diag, jnp.logical_and(yl == k // 2, c == k % 2))

        @pl.when(jnp.logical_not(to_here))
        def _():
            sum_x(k).wait_send()

    @pl.when(diag)
    def _():
        ref = XG.reshape(32, 32, 2048).at[pl.ds(0, 24)]
        local(ref, ref, video_send.at[2]).wait()
        ref = YS.at[pl.ds(0, 7)]
        local(ref, ref, out_send.at[7]).wait()


def block(
    video,
    video_length,
    prompt,
    prompt_length,
    prompt_choice,
    ffn_gain,
    ffn_gate,
    ffn_up,
    ffn_down,
    final_gain,
    video_gain,
    w_query,
    w_key,
    w_value,
    w_text_key,
    w_text_value,
    w_out,
):
    smem = pl.BlockSpec(memory_space=pltpu.SMEM)
    vmem = pl.BlockSpec(memory_space=pltpu.VMEM)
    hbm = pl.BlockSpec(memory_space=pl.ANY)
    dma = pltpu.SemaphoreType.DMA
    width, half = 4096, 2048
    return pl.pallas_call(
        kernel,
        out_shape=jax.ShapeDtypeStruct(video.shape, video.dtype),
        in_specs=[smem] * 3 + [vmem] * 5 + [hbm] * 9,
        out_specs=vmem,
        scratch_shapes=[
            pltpu.VMEM((6, 16, 256, 256), BF),
            pltpu.VMEM((16, 8, width), BF),
            pltpu.VMEM((8, width), BF),
            pltpu.VMEM((16, 8, width), BF),
            pltpu.VMEM((128, width), BF),
            pltpu.VMEM(ffn_gate.shape, BF),
            pltpu.VMEM(ffn_up.shape, BF),
            pltpu.VMEM(ffn_down.shape, BF),
            pltpu.VMEM((128, 384), F32),
            pltpu.VMEM((128, 384), F32),
            pltpu.VMEM((128, 384), BF),
            pltpu.VMEM((16, 8, width), BF),
            pltpu.VMEM((16, 8, width), BF),
            pltpu.VMEM((8, width), BF),
            pltpu.VMEM((16, 8, width), BF),
            pltpu.VMEM((2, 32, half), BF),
            pltpu.VMEM((2, 16, 32, half), BF),
            pltpu.VMEM((512, 256), F32),
            pltpu.VMEM((512, 256), F32),
            pltpu.VMEM((512, 256), F32),
            pltpu.VMEM((512, 256), BF),
            pltpu.VMEM((640, 256), BF),
            pltpu.VMEM((640, 256), BF),
            pltpu.VMEM((2, 16, 32, half), BF),
            pltpu.VMEM((3, 4, 32, half), BF),
            pltpu.VMEM((3, 8, 32, half), BF),
            pltpu.VMEM((4, 32, half), BF),
            pltpu.VMEM((8, 32, half), BF),
            pltpu.VMEM((2, 4, 32, half), BF),
            pltpu.VMEM((8, 128), jnp.int32),
            pltpu.VMEM((8, 128), jnp.int32),
            dma((3,)),
            dma((7, 8)),
            dma((7,)),
            dma((8,)),
            dma((7,)),
            dma,
            dma((3,)),
            dma((3,)),
            dma((3,)),
            dma((4,)),
            dma((5,)),
            dma((4,)),
            dma((8,)),
        ],
        compiler_params=pltpu.CompilerParams(
            collective_id=0, has_side_effects=True, vmem_limit_bytes=58 * 1024 * 1024
        ),
        name="joint_attention",
    )(
        video_length,
        prompt_length,
        prompt_choice,
        video,
        prompt,
        ffn_gain.reshape(1, -1),
        final_gain.reshape(1, -1),
        video_gain.reshape(1, -1),
        ffn_gate,
        ffn_up,
        ffn_down,
        w_text_key,
        w_text_value,
        w_query,
        w_key,
        w_value,
        w_out,
    )


def solution(mesh):
    in_specs = (
        P("vid", "seq", None),
        P("vid"),
        P("vid", "seq", None),
        P(),
        P("vid"),
        P(),
        P(None, "seq"),
        P(None, "seq"),
        P("seq", None),
        P(),
        P(),
        P("vid", "seq"),
        P("vid", "seq"),
        P("vid", "seq"),
        P("vid", "seq"),
        P("vid", "seq"),
        P("seq", "vid"),
    )
    out_specs = P("vid", "seq", None)
    return jax.shard_map(block, mesh=mesh, in_specs=in_specs, out_specs=out_specs, check_vma=False)
```

```python
import jax
import jax.numpy as jnp
from jax import lax
from jax.experimental import pallas as pl
from jax.experimental.pallas import tpu as pltpu
from jax.sharding import PartitionSpec as P

HD = 128
EPSILON = 1e-06
MESH = pl.DeviceIdType.MESH
BF = jnp.bfloat16
F32 = jnp.float32

TK, TV, Q, K, V, O, PROMPT = range(7)


def rms_norm(values, gain):
    return values * lax.rsqrt(jnp.mean(values * values, axis=-1, keepdims=True) + EPSILON) * gain


def kernel(
    length_ref,
    prompt_length_ref,
    choice_ref,
    video_ref,
    prompt_ref,
    ffn_gain_ref,
    final_gain_ref,
    video_gain_ref,
    gate_hbm,
    up_hbm,
    down_hbm,
    w_text_key,
    w_text_value,
    w_query,
    w_key,
    w_value,
    w_out,
    out_ref,
    W,
    PB,
    SEL,
    PG,
    FN,
    gate_ref,
    up_ref,
    down_ref,
    gate_acc,
    up_acc,
    hidden,
    FP,
    FS,
    FQ,
    FR,
    TX,
    TG,
    NV,
    XG,
    q_acc,
    k_acc,
    v_acc,
    queries,
    probs,
    keys,
    values,
    AX,
    OX,
    SB,
    YR,
    YS,
    RR,
    info_own,
    info,
    ffn_sem,
    ring_recv,
    ring_send,
    swap_send,
    sib_recv,
    info_sem,
    group_recv,
    group_send,
    group_send0,
    prompt_sem,
    video_recv,
    video_send,
    out_recv,
    out_send,
    weight_sem,
    weight_recv,
):
    vid, seq = lax.axis_index("vid"), lax.axis_index("seq")
    yh, z = vid // 8, vid % 8
    x, yl, c = seq // 4, (seq // 2) % 2, seq % 2
    y = yh * 2 + yl
    diag = c == yh
    taken = (y + 3) % 4
    head_block = x * 4 + (taken % 2) * 2 + taken // 2
    taker = (yl + 1 + 2 * c) % 4
    taker = ((taker // 2) * 8 + z, x * 4 + (taker % 2) * 2 + yh)
    sibling = (vid, seq + 1 - 2 * c)
    z_right = (yh * 8 + (z + 1) % 8, seq)
    z_left = (yh * 8 + (z + 7) % 8, seq)

    def to_chip(k):
        xk, yk = (x + k // 4) % 4, (y + k % 4) % 4
        return ((yk // 2) * 8 + z, xk * 4 + (yk % 2) * 2 + yh)

    def place(k):
        return ((x + k // 4) % 4) * 4 + ((yl + (k // 2) % 2) % 2) * 2 + (c + k % 2) % 2

    def local(src, dst, sem):
        return pltpu.make_async_copy(src, dst, sem)

    def remote(src, dst, send, recv, device):
        return pltpu.make_async_remote_copy(
            src_ref=src, dst_ref=dst, send_sem=send, recv_sem=recv, device_id=device, device_id_type=MESH
        )

    ffn_copies = [
        local(gate_hbm, gate_ref, ffn_sem.at[0]),
        local(up_hbm, up_ref, ffn_sem.at[1]),
        local(down_hbm, down_ref, ffn_sem.at[2]),
    ]
    for copy in ffn_copies:
        copy.start()

    barrier = pltpu.get_barrier_semaphore()

    def greet(k, carry):
        seq_k = (seq + k) % 16
        vid_k = ((yh + k // 16) % 2) * 8 + z
        pl.semaphore_signal(barrier, inc=1, device_id=(vid_k, seq_k), device_id_type=MESH)
        return carry

    lax.fori_loop(1, 32, greet, 0)
    for neighbour in (z_left, z_right):
        pl.semaphore_signal(barrier, inc=1, device_id=neighbour, device_id_type=MESH)

    choice = choice_ref[0]
    row = lax.broadcasted_iota(jnp.int32, (8, 128), 0)
    text_live = prompt_length_ref[choice]
    info_own[...] = jnp.where(row == 0, choice, jnp.where(row == 1, length_ref[0], text_live))

    normed = rms_norm(video_ref[0].astype(F32), video_gain_ref[...]).astype(BF)
    NV[0] = normed[:, :2048]
    NV[1] = normed[:, 2048:]

    pl.semaphore_wait(barrier, 33)

    sources = [w_text_key, w_text_value, w_query, w_key, w_value, w_out, prompt_ref.at[0]]

    def slot(w, block):
        return PB.at[block] if w == PROMPT else W.at[w, block]

    def swap_copy(w):
        return remote(sources[w], slot(w, yh * 8 + z), swap_send.at[w], ring_recv.at[w, z], taker)

    info_copy = remote(info_own, info, swap_send.at[7], info_sem, taker)
    swap_copy(PROMPT).start()
    info_copy.start()

    def swap(w):
        swap_copy(w).start()

    def ring_wait(w, zz):
        ref = slot(w, c * 8 + zz)
        local(ref, ref, ring_recv.at[w, zz]).wait()

    def ring_to(w, zz, device):
        ref = slot(w, c * 8 + zz)
        remote(ref, ref, ring_send.at[w], ring_recv.at[w, zz], device).start()

    def to_sibling(w, zz):
        if w in (O, PROMPT):
            return
        ref = slot(w, c * 8 + zz)
        remote(ref, ref, ring_send.at[w], sib_recv.at[w], sibling).start()

    def own(w):
        ring_wait(w, z)
        ring_to(w, z, z_right)
        ring_to(w, z, z_left)
        to_sibling(w, z)

    def hop(w, k):
        right_hops = 4 if w % 2 == 0 else 3
        left_hops = 7 - right_hops
        from_left, from_right = (z + 8 - k) % 8, (z + k) % 8
        if k <= right_hops:
            ring_wait(w, from_left)
            if k < right_hops:
                ring_to(w, from_left, z_right)
        if k <= left_hops:
            ring_wait(w, from_right)
            if k < left_hops:
                ring_to(w, from_right, z_left)
        if k <= right_hops:
            to_sibling(w, from_left)
        if k <= left_hops:
            to_sibling(w, from_right)

    def sibling_wait(w):
        ref = W.at[w, pl.ds(0, 8)]
        local(ref, ref, sib_recv.at[w]).wait()

    not_diag = jnp.logical_not(diag)

    def at_core(xk, yk, core):
        return ((yk // 2) * 8 + z, xk * 4 + (yk % 2) * 2 + core)

    def video_slot(h):
        return XG.at[h, x, yl, c]

    def video_x(k):
        return remote(
            NV.at[0], video_slot(0), video_send.at[0], video_recv.at[0], at_core((x + k) % 4, y, yh)
        )

    def video_y(k):
        return remote(
            NV.at[1], video_slot(1), video_send.at[1], video_recv.at[1], at_core(x, (y + k) % 4, yh)
        )

    own_chip = [
        remote(
            NV.at[h], video_slot(h), video_send.at[4], video_recv.at[h], sibling
        )
        for h in range(2)
    ]

    @pl.when(diag)
    def _():
        for h in range(2):
            local(NV.at[h], video_slot(h), video_recv.at[h]).start()

    @pl.when(not_diag)
    def _():
        for h in range(2):
            own_chip[h].start()

    def send_lower():
        for k in (2, 1, 3):
            video_x(k).start()

    def send_upper():
        for k in (2, 1, 3):
            video_y(k).start()

    def lower_on(k):
        ref = XG.at[0, :, yl]
        return remote(ref, ref, video_send.at[2], video_recv.at[2], at_core(x, (y + k) % 4, c))

    def upper_on(k):
        ref = XG.at[1, x]
        return remote(ref, ref, video_send.at[3], video_recv.at[3], at_core((x + k) % 4, y, c))

    def pass_upper_on():
        ref = XG.at[1, 0]
        local(ref, ref, video_recv.at[1]).wait()
        for k in (2, 1, 3):
            upper_on(k).start()

    def pass_lower_on():
        @pl.when(diag)
        def _():
            ref = XG.at[0, pl.ds(0, 2)]
            local(ref, ref, video_recv.at[0]).wait()
            for k in (2, 1, 3):
                lower_on(k).start()

    def video_wait():
        ref = XG.at[1, pl.ds(0, 3)]
        local(ref, ref, video_recv.at[3]).wait()

        @pl.when(diag)
        def _():
            ref = XG.at[0, pl.ds(0, 2)]
            local(ref, ref, video_recv.at[2]).wait()

        @pl.when(not_diag)
        def _():
            ref = XG.at[0]
            local(ref, ref, video_recv.at[2]).wait()

    PROMPTS, SUMS, TEXT = range(3)

    def send_prompt(k):
        device = (c * 8 + z, ((x + k // 2) % 4) * 4 + ((yl + k % 2) % 2) * 2 + x // 2)
        return remote(SEL, PG.at[head_block], group_send.at[PROMPTS], group_recv.at[PROMPTS], device)

    half_chosen = PG.at[pl.ds(pl.multiple_of(c * 8, 8), 8)]
    pass_chosen = remote(half_chosen, half_chosen, prompt_sem.at[2], prompt_sem.at[3], sibling)

    def pass_chosen_on():
        local(half_chosen, half_chosen, group_recv.at[PROMPTS]).wait()
        pass_chosen.start()

    def spread(first, last, make):
        def step(k, carry):
            make(k).start()
            return carry

        lax.fori_loop(first, last, step, 0)

    def first_send(copy, copy_local, group):
        @pl.when(diag)
        def _():
            copy_local.start()

        @pl.when(jnp.logical_not(diag))
        def _():
            copy.start()

    prompt0 = remote(
        SEL,
        PG.at[head_block],
        group_send0.at[PROMPTS],
        group_recv.at[PROMPTS],
        (c * 8 + z, x * 4 + yl * 2 + x // 2),
    )
    chosen_here = jnp.logical_and(diag, c == x // 2)

    def send_prompts():
        ring_wait(PROMPT, z)
        ref = PB.at[c * 8 + z]

        def step(k, carry):
            remote(
                ref, ref, ring_send.at[PROMPT], sib_recv.at[PROMPT], (yh * 8 + (z + k) % 8, seq)
            ).start()
            return carry

        lax.fori_loop(1, 8, step, 0)

    half_prompts = PB.at[pl.ds(pl.multiple_of(c * 8, 8), 8)]
    pass_prompts = remote(half_prompts, half_prompts, prompt_sem.at[0], prompt_sem.at[1], sibling)

    def pass_prompts_on():
        ref = PB.at[pl.ds(0, 7)]
        local(ref, ref, sib_recv.at[PROMPT]).wait()
        pass_prompts.start()

    def choose_prompt():
        pass_prompts.wait_recv()
        local(info, info, info_sem).wait()
        wanted = info[0:1, 0:1]

        def pick(i, total):
            return total + jnp.where(wanted == i, PB[i].astype(F32), 0.0)

        SEL[...] = lax.fori_loop(0, 16, pick, jnp.zeros(SEL.shape, F32)).astype(BF)

        @pl.when(chosen_here)
        def _():
            local(SEL, PG.at[head_block], group_recv.at[PROMPTS]).start()

        @pl.when(jnp.logical_not(chosen_here))
        def _():
            prompt0.start()

        spread(1, 8, send_prompt)

    def norm_rows(i, carry):
        rows = PG[pl.ds(2 * i, 2)].astype(F32).reshape(16, PG.shape[2])
        FN[pl.ds(pl.multiple_of(i * 16, 16), 16), :] = rms_norm(rows, ffn_gain_ref[...]).astype(BF)
        return carry

    def gate_up(i, carry):
        at = pl.ds(pl.multiple_of(i * 512, 512), 512)
        rows = FN[:, at]
        gate_acc[...] += jnp.dot(rows, gate_ref[at, :], preferred_element_type=F32)
        up_acc[...] += jnp.dot(rows, up_ref[at, :], preferred_element_type=F32)
        return carry

    def ffn_up():
        pass_chosen.wait_recv()
        lax.fori_loop(0, 8, norm_rows, 0)
        ffn_copies[0].wait()
        ffn_copies[1].wait()
        gate_acc[...] = jnp.zeros_like(gate_acc)
        up_acc[...] = jnp.zeros_like(up_acc)
        lax.fori_loop(0, 8, gate_up, 0)
        hidden[...] = (jax.nn.gelu(gate_acc[...], approximate=True) * up_acc[...]).astype(BF)

    def down_proj(i, carry):
        at = pl.ds(pl.multiple_of(i * 256, 256), 256)
        part = jnp.dot(hidden[...], down_ref[:, at], preferred_element_type=F32)
        FP[:, :, :, at] = part.reshape(8, 2, 8, 256).astype(BF)
        return carry

    pass_sums = remote(FP.at[:, 1 - c], FS, prompt_sem.at[4], prompt_sem.at[5], sibling)
    own_chip_index = seq // 2

    def send_sums(k):
        to = ((x + k // 2) % 4) * 2 + (yl + k % 2) % 2
        return remote(
            FQ.at[to], FR.at[own_chip_index], group_send.at[SUMS], group_recv.at[SUMS], (vid, to * 2 + c)
        )

    def ffn_down():
        ffn_copies[2].wait()
        lax.fori_loop(0, 16, down_proj, 0)
        pass_sums.start()

    def ffn_sums():
        pass_sums.wait_recv()

        def step(i, carry):
            FQ[i] = (FP[i, c].astype(F32) + FS[i].astype(F32)).astype(BF)
            return carry

        lax.fori_loop(0, 8, step, 0)
        local(FQ.at[own_chip_index], FR.at[own_chip_index], group_recv.at[SUMS]).start()
        spread(1, 8, send_sums)

    def send_text(k):
        return remote(TX, TG.at[seq], group_send.at[TEXT], group_recv.at[TEXT], to_chip(k))

    text0 = remote(TX, TG.at[seq], group_send0.at[TEXT], group_recv.at[TEXT], to_chip(0))

    def text_rows():
        local(FR, FR, group_recv.at[SUMS]).wait()
        encoded = lax.fori_loop(
            0, 8, lambda i, total: total + FR[i].astype(F32), jnp.zeros(TX.shape, F32)
        )
        encoded = PG[seq].astype(F32) + encoded
        TX[...] = rms_norm(encoded, final_gain_ref[...]).astype(BF)
        first_send(text0, local(TX, TG.at[seq], group_recv.at[TEXT]), TEXT)
        spread(1, 16, send_text)

    def video_rows(j):
        at = pl.ds(pl.multiple_of((j % 8) * 256, 256), 256)
        return XG[j // 8, :, :, :, :, at].reshape(512, 256)

    def project(w, acc, result):
        sibling_wait(w)
        acc[...] = jnp.zeros_like(acc)

        def step(j, carry):
            acc[...] += jnp.dot(video_rows(j), W[w, j], preferred_element_type=F32)
            return carry

        lax.fori_loop(0, 16, step, 0)
        result[pl.ds(0, 512), :] = acc[...].astype(BF)

    def text_key_value(j, carry):
        at = pl.ds(pl.multiple_of(j * 256, 256), 256)
        rows = TG[:, :, at].astype(F32).reshape(128, 256).astype(BF)
        key_sum, value_sum = carry
        key_sum = key_sum + jnp.dot(rows, W[TK, j], preferred_element_type=F32)
        value_sum = value_sum + jnp.dot(rows, W[TV, j], preferred_element_type=F32)
        return key_sum, value_sum

    def text_projections():
        local(TG, TG, group_recv.at[TEXT]).wait()
        sibling_wait(TK)
        sibling_wait(TV)
        zero = jnp.zeros((128, 256), F32)
        text_key, text_value = lax.fori_loop(0, 16, text_key_value, (zero, zero))
        keys[pl.ds(512, 128), :] = text_key.astype(BF)
        values[pl.ds(512, 128), :] = text_value.astype(BF)

    mine = x // 2 == c

    def weight_copy(i):
        xk = 2 * c + i
        return remote(
            W.at[O, pl.ds(pl.multiple_of(xk * 4, 4), 4)], OX.at[x], weight_sem.at[i], weight_recv, at_core(xk, y, c)
        )

    def send_weights():
        for i in range(2):

            @pl.when(x != 2 * c + i)
            def _():
                weight_copy(i).start()

            @pl.when(x == 2 * c + i)
            def _():
                local(W.at[O, pl.ds(pl.multiple_of(x * 4, 4), 4)], OX.at[x], weight_recv).start()

    pass_weights = remote(OX, OX, weight_sem.at[2], weight_sem.at[3], sibling)

    def pass_weights_on():
        @pl.when(mine)
        def _():
            local(OX, OX, weight_recv).wait()
            pass_weights.start()

    def weights_wait():
        @pl.when(jnp.logical_not(mine))
        def _():
            pass_weights.wait_recv()

    def attended_x(part, xk):
        ref = AX.at[x, part]
        return remote(ref, ref, out_send.at[0], out_recv.at[part], at_core(xk, y, c))

    def out_y(part, k):
        return remote(
            SB.at[pl.ds(part * 4 + k * 2, 2)],
            YR.at[(y + 3 - (c * 2 + k)) % 4, pl.ds(part * 2, 2)],
            out_send.at[1 + k],
            out_recv.at[4 + part],
            at_core(x, c * 2 + k, c),
        )

    def sum_y(xk, core):
        return remote(
            YS.at[xk * 2 + core], RR.at[x], out_send.at[3], out_recv.at[8], at_core(xk, y, core)
        )

    def attention_probs(first, last):
        position = lax.broadcasted_iota(jnp.int32, (1, 640), 1)
        live = position < jnp.where(position < 512, info[1:2, 0:1], info[2:3, 0:1] + 512)

        def step(i, carry):
            part = (x + 1 + i) % 4
            rows = pl.ds(pl.multiple_of(part * 128, 128), 128)
            for h in range(2):
                lanes = pl.ds(h * HD, HD)
                scores = lax.dot_general(
                    queries[rows, lanes], keys[:, lanes], (((1,), (1,)), ((), ())), preferred_element_type=F32
                )
                scores = jnp.where(live, scores * HD ** (-0.5), -1e30)
                e = jnp.exp(scores - jnp.max(scores, axis=-1, keepdims=True))
                probs[part, h] = (e / jnp.sum(e, axis=-1, keepdims=True)).astype(BF)
            return carry

        lax.fori_loop(first, last, step, 0)

    def attend(part, carry):
        for h in range(2):
            lanes = pl.ds(h * HD, HD)
            AX[x, part, :, lanes] = jnp.dot(
                probs[part, h], values[:, lanes], preferred_element_type=F32
            ).astype(BF)
        return carry

    def attend_all():
        lax.fori_loop(0, 4, attend, 0)

        def step(i, carry):
            for k in (2, 1, 3):
                xk = (x + k) % 4
                attended_x((xk + 1 + i) % 4, xk).start()
            return carry

        lax.fori_loop(0, 4, step, 0)

    def project_part(i, carry):
        part = (x + 1 + i) % 4
        ref = AX.at[pl.ds(0, 3), 0]
        local(ref, ref, out_recv.at[part]).wait()
        for m in range(4):
            total = jnp.dot(AX[0, part], OX[0, m], preferred_element_type=F32)
            for j in range(1, 4):
                total = total + jnp.dot(AX[j, part], OX[j, m], preferred_element_type=F32)
            SB[pl.ds(part * 4, 4), :, pl.ds(m * 256, 256)] = total.reshape(4, 32, 256).astype(BF)
        for k in range(2):

            @pl.when(y != c * 2 + k)
            def _():
                out_y(part, k).start()

        return carry

    def sum_part(i, carry):
        part = (x + 1 + i) % 4
        ref = YR.at[pl.ds(0, 3), pl.ds(0, 2)]
        local(ref, ref, out_recv.at[4 + part]).wait()
        for step in range(2):
            core = (c + 1 + step) % 2
            total = SB[part * 4 + yl * 2 + core].astype(F32)
            for j in range(3):
                total = total + YR[j, part * 2 + core].astype(F32)
            YS[part * 2 + core] = total.astype(BF)
            to_here = jnp.logical_and(part == x, core == c)

            @pl.when(jnp.logical_not(to_here))
            def _():
                sum_y(part, core).start()

            @pl.when(to_here)
            def _():
                local(YS.at[part * 2 + core], RR.at[x], out_recv.at[8]).start()

        return carry

    send_lower()
    swap(TK)
    send_upper()
    own(PROMPT)
    swap(TV)
    own(TK)
    hop(PROMPT, 1)
    swap(O)
    own(TV)
    hop(PROMPT, 2)
    swap(Q)
    hop(PROMPT, 3)
    own(O)
    swap(K)
    hop(PROMPT, 4)
    pass_prompts.start()
    own(Q)
    hop(TK, 1)
    choose_prompt()
    swap(V)
    hop(TV, 1)
    hop(O, 1)
    hop(Q, 1)
    own(K)
    own(V)
    pass_chosen_on()
    pass_upper_on()
    pass_lower_on()
    ffn_up()
    hop(TK, 2)
    hop(TV, 2)
    hop(O, 2)
    hop(Q, 2)
    hop(K, 1)
    ffn_down()
    hop(V, 1)
    hop(TK, 3)
    ffn_sums()
    hop(TV, 3)
    hop(O, 3)
    hop(Q, 3)
    hop(K, 2)
    hop(V, 2)
    text_rows()
    hop(TK, 4)
    hop(TV, 4)
    hop(O, 4)
    hop(Q, 4)
    hop(K, 3)
    hop(V, 3)
    send_weights()
    video_wait()
    project(Q, q_acc, queries)
    hop(K, 4)
    project(K, k_acc, keys)
    text_projections()
    attention_probs(0, 4)
    pass_weights_on()
    hop(V, 4)
    project(V, v_acc, values)
    attend_all()
    weights_wait()
    lax.fori_loop(0, 4, project_part, 0)

    @pl.when(diag)
    def _():
        lax.fori_loop(0, 4, sum_part, 0)

    local(RR, RR, out_recv.at[8]).wait()
    row_position = seq * 32 + lax.broadcasted_iota(jnp.int32, (32, 1), 0)
    row_live = row_position < length_ref[0]

    for j in range(4):
        at = pl.ds(j * 1024, 1024)
        updated = video_ref[0, :, at].astype(F32) + jnp.where(row_live, RR[j].astype(F32), 0.0)
        out_ref[0, :, at] = updated.astype(BF)

    for w in range(7):
        swap_copy(w).wait_send()
    info_copy.wait_send()

    @pl.when(jnp.logical_not(diag))
    def _():
        text0.wait_send()
        both = XG.at[0, 0, 0]
        local(both, both, video_send.at[4]).wait()

    pass_prompts.wait_send()
    for w in range(7):
        ref = PB.at[pl.ds(0, 7)] if w == PROMPT else W.at[w, pl.ds(0, 7 if w == O else 15)]
        local(ref, ref, ring_send.at[w]).wait()
    @pl.when(jnp.logical_not(chosen_here))
    def _():
        prompt0.wait_send()

    pass_chosen.wait_send()
    pass_sums.wait_send()
    for group, buffer in ((PROMPTS, PG), (SUMS, FR), (TEXT, TG)):
        ref = buffer.at[pl.ds(0, 15 if group == TEXT else 7)]
        local(ref, ref, group_send.at[group]).wait()
    for sem in (video_send.at[0], video_send.at[1]):
        ref = XG.at[0, pl.ds(0, 3), 0, 0]
        local(ref, ref, sem).wait()
    ref = XG.at[0, pl.ds(0, 3)]
    local(ref, ref, video_send.at[3]).wait()
    ref = AX.at[pl.ds(0, 3)]
    local(ref, ref, out_send.at[0]).wait()
    for k in range(2):

        @pl.when(x != 2 * c + k)
        def _():
            weight_copy(k).wait_send()

        @pl.when(y != c * 2 + k)
        def _():
            ref = SB.at[pl.ds(0, 8)]
            local(ref, ref, out_send.at[1 + k]).wait()

    @pl.when(mine)
    def _():
        pass_weights.wait_send()

    @pl.when(diag)
    def _():
        ref = XG.at[:, pl.ds(0, 3)]
        local(ref, ref, video_send.at[2]).wait()
        ref = YS.at[pl.ds(0, 7)]
        local(ref, ref, out_send.at[3]).wait()


def block(
    video,
    video_length,
    prompt,
    prompt_length,
    prompt_choice,
    ffn_gain,
    ffn_gate,
    ffn_up,
    ffn_down,
    final_gain,
    video_gain,
    w_query,
    w_key,
    w_value,
    w_text_key,
    w_text_value,
    w_out,
):
    smem = pl.BlockSpec(memory_space=pltpu.SMEM)
    vmem = pl.BlockSpec(memory_space=pltpu.VMEM)
    hbm = pl.BlockSpec(memory_space=pl.ANY)
    dma = pltpu.SemaphoreType.DMA
    width, half, quarter = 4096, 2048, 1024
    return pl.pallas_call(
        kernel,
        out_shape=jax.ShapeDtypeStruct(video.shape, video.dtype),
        in_specs=[smem] * 3 + [vmem] * 5 + [hbm] * 9,
        out_specs=vmem,
        scratch_shapes=[
            pltpu.VMEM((6, 16, 256, 256), BF),
            pltpu.VMEM((16, 8, width), BF),
            pltpu.VMEM((8, width), BF),
            pltpu.VMEM((16, 8, width), BF),
            pltpu.VMEM((128, width), BF),
            pltpu.VMEM(ffn_gate.shape, BF),
            pltpu.VMEM(ffn_up.shape, BF),
            pltpu.VMEM(ffn_down.shape, BF),
            pltpu.VMEM((128, 384), F32),
            pltpu.VMEM((128, 384), F32),
            pltpu.VMEM((128, 384), BF),
            pltpu.VMEM((8, 2, 8, width), BF),
            pltpu.VMEM((8, 8, width), BF),
            pltpu.VMEM((8, 8, width), BF),
            pltpu.VMEM((8, 8, width), BF),
            pltpu.VMEM((8, width), BF),
            pltpu.VMEM((16, 8, width), BF),
            pltpu.VMEM((2, 32, half), BF),
            pltpu.VMEM((2, 4, 2, 2, 32, half), BF),
            pltpu.VMEM((512, 256), F32),
            pltpu.VMEM((512, 256), F32),
            pltpu.VMEM((512, 256), F32),
            pltpu.VMEM((512, 256), BF),
            pltpu.VMEM((4, 2, 128, 640), BF),
            pltpu.VMEM((640, 256), BF),
            pltpu.VMEM((640, 256), BF),
            pltpu.VMEM((4, 4, 128, 256), BF),
            pltpu.VMEM((4, 4, 256, 256), BF),
            pltpu.VMEM((16, 32, quarter), BF),
            pltpu.VMEM((3, 8, 32, quarter), BF),
            pltpu.VMEM((8, 32, quarter), BF),
            pltpu.VMEM((4, 32, quarter), BF),
            pltpu.VMEM((8, 128), jnp.int32),
            pltpu.VMEM((8, 128), jnp.int32),
            dma((3,)),
            dma((7, 8)),
            dma((7,)),
            dma((8,)),
            dma((7,)),
            dma,
            dma((3,)),
            dma((3,)),
            dma((3,)),
            dma((6,)),
            dma((4,)),
            dma((5,)),
            dma((9,)),
            dma((5,)),
            dma((4,)),
            dma,
        ],
        compiler_params=pltpu.CompilerParams(
            collective_id=0, has_side_effects=True, vmem_limit_bytes=58 * 1024 * 1024
        ),
        name="joint_attention",
    )(
        video_length,
        prompt_length,
        prompt_choice,
        video,
        prompt,
        ffn_gain.reshape(1, -1),
        final_gain.reshape(1, -1),
        video_gain.reshape(1, -1),
        ffn_gate,
        ffn_up,
        ffn_down,
        w_text_key,
        w_text_value,
        w_query,
        w_key,
        w_value,
        w_out,
    )


def solution(mesh):
    in_specs = (
        P("vid", "seq", None),
        P("vid"),
        P("vid", "seq", None),
        P(),
        P("vid"),
        P(),
        P(None, "seq"),
        P(None, "seq"),
        P("seq", None),
        P(),
        P(),
        P("vid", "seq"),
        P("vid", "seq"),
        P("vid", "seq"),
        P("vid", "seq"),
        P("vid", "seq"),
        P("seq", "vid"),
    )
    out_specs = P("vid", "seq", None)
    return jax.shard_map(block, mesh=mesh, in_specs=in_specs, out_specs=out_specs, check_vma=False)
```

```python
import jax
import jax.numpy as jnp
from jax import lax
from jax.experimental import pallas as pl
from jax.experimental.pallas import tpu as pltpu
from jax.sharding import PartitionSpec as P

HD = 128
EPSILON = 1e-06
MESH = pl.DeviceIdType.MESH
BF = jnp.bfloat16
F32 = jnp.float32

TK, TV, Q, K, V, O, PROMPT = range(7)


def rms_norm(values, gain):
    return values * lax.rsqrt(jnp.mean(values * values, axis=-1, keepdims=True) + EPSILON) * gain


def kernel(
    length_ref,
    prompt_length_ref,
    choice_ref,
    video_ref,
    prompt_ref,
    ffn_gain_ref,
    final_gain_ref,
    video_gain_ref,
    gate_hbm,
    up_hbm,
    down_hbm,
    w_text_key,
    w_text_value,
    w_query,
    w_key,
    w_value,
    w_out,
    out_ref,
    W,
    PB,
    SEL,
    PG,
    FN,
    gate_ref,
    up_ref,
    down_ref,
    gate_acc,
    up_acc,
    hidden,
    FP,
    FS,
    FQ,
    FR,
    TX,
    TG,
    NV,
    XG,
    q_acc,
    k_acc,
    v_acc,
    queries,
    probs,
    keys,
    values,
    AX,
    OX,
    SB,
    YR,
    YS,
    RR,
    info_own,
    info,
    ffn_sem,
    ring_recv,
    ring_send,
    swap_send,
    sib_recv,
    info_sem,
    group_recv,
    group_send,
    group_send0,
    prompt_sem,
    video_recv,
    video_send,
    out_recv,
    out_send,
    weight_sem,
    weight_recv,
):
    vid, seq = lax.axis_index("vid"), lax.axis_index("seq")
    yh, z = vid // 8, vid % 8
    x, yl, c = seq // 4, (seq // 2) % 2, seq % 2
    y = yh * 2 + yl
    diag = c == yh
    taken = (y + 3) % 4
    head_block = x * 4 + (taken % 2) * 2 + taken // 2
    taker = (yl + 1 + 2 * c) % 4
    taker = ((taker // 2) * 8 + z, x * 4 + (taker % 2) * 2 + yh)
    sibling = (vid, seq + 1 - 2 * c)
    z_right = (yh * 8 + (z + 1) % 8, seq)
    z_left = (yh * 8 + (z + 7) % 8, seq)

    def to_chip(k):
        xk, yk = (x + k // 4) % 4, (y + k % 4) % 4
        return ((yk // 2) * 8 + z, xk * 4 + (yk % 2) * 2 + yh)

    def place(k):
        return ((x + k // 4) % 4) * 4 + ((yl + (k // 2) % 2) % 2) * 2 + (c + k % 2) % 2

    def local(src, dst, sem):
        return pltpu.make_async_copy(src, dst, sem)

    def remote(src, dst, send, recv, device):
        return pltpu.make_async_remote_copy(
            src_ref=src, dst_ref=dst, send_sem=send, recv_sem=recv, device_id=device, device_id_type=MESH
        )

    ffn_copies = [
        local(gate_hbm, gate_ref, ffn_sem.at[0]),
        local(up_hbm, up_ref, ffn_sem.at[1]),
        local(down_hbm, down_ref, ffn_sem.at[2]),
    ]
    for copy in ffn_copies:
        copy.start()

    barrier = pltpu.get_barrier_semaphore()

    def greet(k, carry):
        seq_k = (seq + k) % 16
        vid_k = ((yh + k // 16) % 2) * 8 + z
        pl.semaphore_signal(barrier, inc=1, device_id=(vid_k, seq_k), device_id_type=MESH)
        return carry

    lax.fori_loop(1, 32, greet, 0)
    for neighbour in (z_left, z_right):
        pl.semaphore_signal(barrier, inc=1, device_id=neighbour, device_id_type=MESH)

    choice = choice_ref[0]
    row = lax.broadcasted_iota(jnp.int32, (8, 128), 0)
    text_live = prompt_length_ref[choice]
    info_own[...] = jnp.where(row == 0, choice, jnp.where(row == 1, length_ref[0], text_live))

    normed = rms_norm(video_ref[0].astype(F32), video_gain_ref[...]).astype(BF)
    NV[0] = normed[:, :2048]
    NV[1] = normed[:, 2048:]

    pl.semaphore_wait(barrier, 33)

    sources = [w_text_key, w_text_value, w_query, w_key, w_value, w_out, prompt_ref.at[0]]

    def slot(w, block):
        return PB.at[block] if w == PROMPT else W.at[w, block]

    def swap_copy(w):
        return remote(sources[w], slot(w, yh * 8 + z), swap_send.at[w], ring_recv.at[w, z], taker)

    info_copy = remote(info_own, info, swap_send.at[7], info_sem, taker)
    swap_copy(PROMPT).start()
    info_copy.start()

    def swap(w):
        swap_copy(w).start()

    def ring_wait(w, zz):
        ref = slot(w, c * 8 + zz)
        local(ref, ref, ring_recv.at[w, zz]).wait()

    def ring_to(w, zz, device):
        ref = slot(w, c * 8 + zz)
        remote(ref, ref, ring_send.at[w], ring_recv.at[w, zz], device).start()

    def to_sibling(w, zz):
        if w in (O, PROMPT):
            return
        ref = slot(w, c * 8 + zz)
        remote(ref, ref, ring_send.at[w], sib_recv.at[w], sibling).start()

    def own(w):
        ring_wait(w, z)
        ring_to(w, z, z_right)
        ring_to(w, z, z_left)
        to_sibling(w, z)

    def hop(w, k):
        right_hops = 4 if w % 2 == 0 else 3
        left_hops = 7 - right_hops
        from_left, from_right = (z + 8 - k) % 8, (z + k) % 8
        if k <= right_hops:
            ring_wait(w, from_left)
            if k < right_hops:
                ring_to(w, from_left, z_right)
        if k <= left_hops:
            ring_wait(w, from_right)
            if k < left_hops:
                ring_to(w, from_right, z_left)
        if k <= right_hops:
            to_sibling(w, from_left)
        if k <= left_hops:
            to_sibling(w, from_right)

    def sibling_wait(w):
        ref = W.at[w, pl.ds(0, 8)]
        local(ref, ref, sib_recv.at[w]).wait()

    not_diag = jnp.logical_not(diag)

    def at_core(xk, yk, core):
        return ((yk // 2) * 8 + z, xk * 4 + (yk % 2) * 2 + core)

    def video_slot(h):
        return XG.at[h, x, yl, c]

    def video_x(k):
        return remote(
            NV.at[0], video_slot(0), video_send.at[0], video_recv.at[0], at_core((x + k) % 4, y, yh)
        )

    def video_y(k):
        return remote(
            NV.at[1], video_slot(1), video_send.at[1], video_recv.at[1], at_core(x, (y + k) % 4, yh)
        )

    own_chip = [
        remote(
            NV.at[h], video_slot(h), video_send.at[4], video_recv.at[h], sibling
        )
        for h in range(2)
    ]

    def keep_video(h):
        @pl.when(diag)
        def _():
            local(NV.at[h], video_slot(h), video_recv.at[h]).start()

        @pl.when(not_diag)
        def _():
            own_chip[h].start()

    def send_lower():
        keep_video(0)
        for k in (2, 1, 3):
            video_x(k).start()

    def send_upper():
        keep_video(1)
        for k in (2, 1, 3):
            video_y(k).start()

    def lower_on(k):
        ref = XG.at[0, :, yl]
        return remote(ref, ref, video_send.at[2], video_recv.at[2], at_core(x, (y + k) % 4, c))

    def upper_on(k):
        ref = XG.at[1, x]
        return remote(ref, ref, video_send.at[3], video_recv.at[3], at_core((x + k) % 4, y, c))

    def pass_upper_on():
        ref = XG.at[1, 0]
        local(ref, ref, video_recv.at[1]).wait()
        for k in (2, 1, 3):
            upper_on(k).start()

    def pass_lower_on():
        @pl.when(diag)
        def _():
            ref = XG.at[0, pl.ds(0, 2)]
            local(ref, ref, video_recv.at[0]).wait()
            for k in (2, 1, 3):
                lower_on(k).start()

    def video_wait():
        ref = XG.at[1, pl.ds(0, 3)]
        local(ref, ref, video_recv.at[3]).wait()

        @pl.when(diag)
        def _():
            ref = XG.at[0, pl.ds(0, 2)]
            local(ref, ref, video_recv.at[2]).wait()

        @pl.when(not_diag)
        def _():
            ref = XG.at[0]
            local(ref, ref, video_recv.at[2]).wait()

    PROMPTS, SUMS, TEXT = range(3)

    def send_prompt(k):
        device = (c * 8 + z, ((x + k // 2) % 4) * 4 + ((yl + k % 2) % 2) * 2 + x // 2)
        return remote(SEL, PG.at[head_block], group_send.at[PROMPTS], group_recv.at[PROMPTS], device)

    half_chosen = PG.at[pl.ds(pl.multiple_of(c * 8, 8), 8)]
    pass_chosen = remote(half_chosen, half_chosen, prompt_sem.at[2], prompt_sem.at[3], sibling)

    def pass_chosen_on():
        local(half_chosen, half_chosen, group_recv.at[PROMPTS]).wait()
        pass_chosen.start()

    def spread(first, last, make):
        def step(k, carry):
            make(k).start()
            return carry

        lax.fori_loop(first, last, step, 0)

    def first_send(copy, copy_local, group):
        @pl.when(diag)
        def _():
            copy_local.start()

        @pl.when(jnp.logical_not(diag))
        def _():
            copy.start()

    prompt0 = remote(
        SEL,
        PG.at[head_block],
        group_send0.at[PROMPTS],
        group_recv.at[PROMPTS],
        (c * 8 + z, x * 4 + yl * 2 + x // 2),
    )
    chosen_here = jnp.logical_and(diag, c == x // 2)

    def send_prompts():
        ring_wait(PROMPT, z)
        ref = PB.at[c * 8 + z]

        def step(k, carry):
            remote(
                ref, ref, ring_send.at[PROMPT], sib_recv.at[PROMPT], (yh * 8 + (z + k) % 8, seq)
            ).start()
            return carry

        lax.fori_loop(1, 8, step, 0)

    half_prompts = PB.at[pl.ds(pl.multiple_of(c * 8, 8), 8)]
    pass_prompts = remote(half_prompts, half_prompts, prompt_sem.at[0], prompt_sem.at[1], sibling)

    def pass_prompts_on():
        ref = PB.at[pl.ds(0, 7)]
        local(ref, ref, sib_recv.at[PROMPT]).wait()
        pass_prompts.start()

    def choose_prompt():
        pass_prompts.wait_recv()
        local(info, info, info_sem).wait()
        wanted = info[0:1, 0:1]

        def pick(i, total):
            return total + jnp.where(wanted == i, PB[i].astype(F32), 0.0)

        SEL[...] = lax.fori_loop(0, 16, pick, jnp.zeros(SEL.shape, F32)).astype(BF)

        @pl.when(chosen_here)
        def _():
            local(SEL, PG.at[head_block], group_recv.at[PROMPTS]).start()

        @pl.when(jnp.logical_not(chosen_here))
        def _():
            prompt0.start()

        spread(1, 8, send_prompt)

    def norm_rows(i, carry):
        rows = PG[pl.ds(2 * i, 2)].astype(F32).reshape(16, PG.shape[2])
        FN[pl.ds(pl.multiple_of(i * 16, 16), 16), :] = rms_norm(rows, ffn_gain_ref[...]).astype(BF)
        return carry

    def ffn_norm():
        pass_chosen.wait_recv()
        lax.fori_loop(0, 8, norm_rows, 0)

    def ffn_project(weights, acc, copy):
        copy.wait()

        def step(i, total):
            at = pl.ds(pl.multiple_of(i * 512, 512), 512)
            return total + jnp.dot(FN[:, at], weights[at, :], preferred_element_type=F32)

        acc[...] = lax.fori_loop(0, 8, step, jnp.zeros(acc.shape, F32))

    def ffn_gate():
        ffn_project(gate_ref, gate_acc, ffn_copies[0])

    def ffn_up():
        ffn_project(up_ref, up_acc, ffn_copies[1])
        hidden[...] = (jax.nn.gelu(gate_acc[...], approximate=True) * up_acc[...]).astype(BF)

    def down_proj(i, carry):
        at = pl.ds(pl.multiple_of(i * 256, 256), 256)
        part = jnp.dot(hidden[...], down_ref[:, at], preferred_element_type=F32)
        FP[:, :, :, at] = part.reshape(8, 2, 8, 256).astype(BF)
        return carry

    pass_sums = remote(FP.at[:, 1 - c], FS, prompt_sem.at[4], prompt_sem.at[5], sibling)
    own_chip_index = seq // 2

    def send_sums(k):
        to = ((x + k // 2) % 4) * 2 + (yl + k % 2) % 2
        return remote(
            FQ.at[to], FR.at[own_chip_index], group_send.at[SUMS], group_recv.at[SUMS], (vid, to * 2 + c)
        )

    def ffn_down():
        ffn_copies[2].wait()
        lax.fori_loop(0, 16, down_proj, 0)
        pass_sums.start()

    def ffn_sums():
        pass_sums.wait_recv()

        def step(i, carry):
            FQ[i] = (FP[i, c].astype(F32) + FS[i].astype(F32)).astype(BF)
            return carry

        lax.fori_loop(0, 8, step, 0)
        local(FQ.at[own_chip_index], FR.at[own_chip_index], group_recv.at[SUMS]).start()
        spread(1, 8, send_sums)

    def send_text(k):
        return remote(TX, TG.at[seq], group_send.at[TEXT], group_recv.at[TEXT], to_chip(k))

    text0 = remote(TX, TG.at[seq], group_send0.at[TEXT], group_recv.at[TEXT], to_chip(0))

    def text_rows():
        local(FR, FR, group_recv.at[SUMS]).wait()
        encoded = lax.fori_loop(
            0, 8, lambda i, total: total + FR[i].astype(F32), jnp.zeros(TX.shape, F32)
        )
        encoded = PG[seq].astype(F32) + encoded
        TX[...] = rms_norm(encoded, final_gain_ref[...]).astype(BF)
        first_send(text0, local(TX, TG.at[seq], group_recv.at[TEXT]), TEXT)
        spread(1, 16, send_text)

    def video_rows(j):
        at = pl.ds(pl.multiple_of((j % 4) * 512, 512), 512)
        return XG[j // 4, :, :, :, :, at].reshape(512, 512)

    def project(w, acc, result):
        sibling_wait(w)
        acc[...] = jnp.zeros_like(acc)

        def step(j, carry):
            weights = W[w, pl.ds(2 * j, 2)].reshape(512, 256)
            acc[...] += jnp.dot(video_rows(j), weights, preferred_element_type=F32)
            return carry

        lax.fori_loop(0, 8, step, 0)
        result[pl.ds(0, 512), :] = acc[...].astype(BF)

    def text_key_value(j, carry):
        at = pl.ds(pl.multiple_of(j * 256, 256), 256)
        rows = TG[:, :, at].astype(F32).reshape(128, 256).astype(BF)
        key_sum, value_sum = carry
        key_sum = key_sum + jnp.dot(rows, W[TK, j], preferred_element_type=F32)
        value_sum = value_sum + jnp.dot(rows, W[TV, j], preferred_element_type=F32)
        return key_sum, value_sum

    def text_projections():
        local(TG, TG, group_recv.at[TEXT]).wait()
        sibling_wait(TK)
        sibling_wait(TV)
        zero = jnp.zeros((128, 256), F32)
        text_key, text_value = lax.fori_loop(0, 16, text_key_value, (zero, zero))
        keys[pl.ds(512, 128), :] = text_key.astype(BF)
        values[pl.ds(512, 128), :] = text_value.astype(BF)

    mine = x // 2 == c

    def weight_copy(i):
        xk = 2 * c + i
        return remote(
            W.at[O, pl.ds(pl.multiple_of(xk * 4, 4), 4)], OX.at[x], weight_sem.at[i], weight_recv, at_core(xk, y, c)
        )

    def send_weights():
        for i in range(2):

            @pl.when(x != 2 * c + i)
            def _():
                weight_copy(i).start()

            @pl.when(x == 2 * c + i)
            def _():
                local(W.at[O, pl.ds(pl.multiple_of(x * 4, 4), 4)], OX.at[x], weight_recv).start()

    pass_weights = remote(OX, OX, weight_sem.at[2], weight_sem.at[3], sibling)

    def pass_weights_on():
        @pl.when(mine)
        def _():
            local(OX, OX, weight_recv).wait()
            pass_weights.start()

    def weights_wait():
        @pl.when(jnp.logical_not(mine))
        def _():
            pass_weights.wait_recv()

    def attended_x(part, xk):
        ref = AX.at[x, part]
        return remote(ref, ref, out_send.at[0], out_recv.at[part], at_core(xk, y, c))

    def out_y(part, k):
        return remote(
            SB.at[pl.ds(part * 4 + k * 2, 2)],
            YR.at[(y + 3 - (c * 2 + k)) % 4, pl.ds(part * 2, 2)],
            out_send.at[1 + k],
            out_recv.at[4 + part],
            at_core(x, c * 2 + k, c),
        )

    def sum_y(xk, core):
        return remote(
            YS.at[xk * 2 + core], RR.at[x], out_send.at[3], out_recv.at[8], at_core(xk, y, core)
        )

    def attention_probs(first, last):
        position = lax.broadcasted_iota(jnp.int32, (1, 640), 1)
        live = position < jnp.where(position < 512, info[1:2, 0:1], info[2:3, 0:1] + 512)

        def step(i, carry):
            part = (x + 1 + i) % 4
            rows = pl.ds(pl.multiple_of(part * 128, 128), 128)
            for h in range(2):
                lanes = pl.ds(h * HD, HD)
                scores = lax.dot_general(
                    queries[rows, lanes], keys[:, lanes], (((1,), (1,)), ((), ())), preferred_element_type=F32
                )
                scores = jnp.where(live, scores * HD ** (-0.5), -1e30)
                e = jnp.exp(scores - jnp.max(scores, axis=-1, keepdims=True))
                probs[part, h] = (e / jnp.sum(e, axis=-1, keepdims=True)).astype(BF)
            return carry

        lax.fori_loop(first, last, step, 0)

    def attend(part, carry):
        for h in range(2):
            lanes = pl.ds(h * HD, HD)
            AX[x, part, :, lanes] = jnp.dot(
                probs[part, h], values[:, lanes], preferred_element_type=F32
            ).astype(BF)
        return carry

    def attend_all():
        lax.fori_loop(0, 4, attend, 0)

        def step(i, carry):
            for k in (2, 1, 3):
                xk = (x + k) % 4
                attended_x((xk + 1 + i) % 4, xk).start()
            return carry

        lax.fori_loop(0, 4, step, 0)

    def project_part(i, carry):
        part = (x + 1 + i) % 4
        ref = AX.at[pl.ds(0, 3), 0]
        local(ref, ref, out_recv.at[part]).wait()
        for m in range(4):
            total = jnp.dot(AX[0, part], OX[0, m], preferred_element_type=F32)
            for j in range(1, 4):
                total = total + jnp.dot(AX[j, part], OX[j, m], preferred_element_type=F32)
            SB[pl.ds(part * 4, 4), :, pl.ds(m * 256, 256)] = total.reshape(4, 32, 256).astype(BF)
        for k in range(2):

            @pl.when(y != c * 2 + k)
            def _():
                out_y(part, k).start()

        return carry

    def sum_part(i, carry):
        part = (x + 1 + i) % 4
        ref = YR.at[pl.ds(0, 3), pl.ds(0, 2)]
        local(ref, ref, out_recv.at[4 + part]).wait()
        for step in range(2):
            core = (c + 1 + step) % 2
            total = SB[part * 4 + yl * 2 + core].astype(F32)
            for j in range(3):
                total = total + YR[j, part * 2 + core].astype(F32)
            YS[part * 2 + core] = total.astype(BF)
            to_here = jnp.logical_and(part == x, core == c)

            @pl.when(jnp.logical_not(to_here))
            def _():
                sum_y(part, core).start()

            @pl.when(to_here)
            def _():
                local(YS.at[part * 2 + core], RR.at[x], out_recv.at[8]).start()

        return carry

    send_lower()
    swap(TK)
    send_upper()
    own(PROMPT)
    swap(TV)
    own(TK)
    hop(PROMPT, 1)
    swap(O)
    own(TV)
    hop(PROMPT, 2)
    swap(Q)
    hop(PROMPT, 3)
    own(O)
    swap(K)
    hop(PROMPT, 4)
    pass_prompts.start()
    swap(V)
    own(Q)
    hop(TK, 1)
    choose_prompt()
    hop(TV, 1)
    hop(O, 1)
    hop(Q, 1)
    own(K)
    own(V)
    pass_chosen_on()
    pass_upper_on()
    pass_lower_on()
    ffn_norm()
    ffn_gate()
    ffn_up()
    hop(TK, 2)
    hop(TV, 2)
    hop(O, 2)
    hop(Q, 2)
    hop(K, 1)
    ffn_down()
    hop(V, 1)
    hop(TK, 3)
    ffn_sums()
    hop(TV, 3)
    hop(O, 3)
    hop(Q, 3)
    hop(K, 2)
    hop(V, 2)
    text_rows()
    hop(TK, 4)
    hop(TV, 4)
    hop(O, 4)
    hop(Q, 4)
    hop(K, 3)
    video_wait()
    project(Q, q_acc, queries)
    hop(V, 3)
    hop(K, 4)
    send_weights()
    project(K, k_acc, keys)
    hop(V, 4)
    text_projections()
    attention_probs(0, 4)
    pass_weights_on()
    project(V, v_acc, values)
    attend_all()
    weights_wait()
    lax.fori_loop(0, 4, project_part, 0)

    @pl.when(diag)
    def _():
        lax.fori_loop(0, 4, sum_part, 0)

    local(RR, RR, out_recv.at[8]).wait()
    row_position = seq * 32 + lax.broadcasted_iota(jnp.int32, (32, 1), 0)
    row_live = row_position < length_ref[0]

    for j in range(4):
        at = pl.ds(j * 1024, 1024)
        updated = video_ref[0, :, at].astype(F32) + jnp.where(row_live, RR[j].astype(F32), 0.0)
        out_ref[0, :, at] = updated.astype(BF)

    for w in range(7):
        swap_copy(w).wait_send()
    info_copy.wait_send()

    @pl.when(jnp.logical_not(diag))
    def _():
        text0.wait_send()
        both = XG.at[0, 0, 0]
        local(both, both, video_send.at[4]).wait()

    pass_prompts.wait_send()
    for w in range(7):
        ref = PB.at[pl.ds(0, 7)] if w == PROMPT else W.at[w, pl.ds(0, 7 if w == O else 15)]
        local(ref, ref, ring_send.at[w]).wait()
    @pl.when(jnp.logical_not(chosen_here))
    def _():
        prompt0.wait_send()

    pass_chosen.wait_send()
    pass_sums.wait_send()
    for group, buffer in ((PROMPTS, PG), (SUMS, FR), (TEXT, TG)):
        ref = buffer.at[pl.ds(0, 15 if group == TEXT else 7)]
        local(ref, ref, group_send.at[group]).wait()
    for sem in (video_send.at[0], video_send.at[1]):
        ref = XG.at[0, pl.ds(0, 3), 0, 0]
        local(ref, ref, sem).wait()
    ref = XG.at[0, pl.ds(0, 3)]
    local(ref, ref, video_send.at[3]).wait()
    ref = AX.at[pl.ds(0, 3)]
    local(ref, ref, out_send.at[0]).wait()
    for k in range(2):

        @pl.when(x != 2 * c + k)
        def _():
            weight_copy(k).wait_send()

        @pl.when(y != c * 2 + k)
        def _():
            ref = SB.at[pl.ds(0, 8)]
            local(ref, ref, out_send.at[1 + k]).wait()

    @pl.when(mine)
    def _():
        pass_weights.wait_send()

    @pl.when(diag)
    def _():
        ref = XG.at[:, pl.ds(0, 3)]
        local(ref, ref, video_send.at[2]).wait()
        ref = YS.at[pl.ds(0, 7)]
        local(ref, ref, out_send.at[3]).wait()


def block(
    video,
    video_length,
    prompt,
    prompt_length,
    prompt_choice,
    ffn_gain,
    ffn_gate,
    ffn_up,
    ffn_down,
    final_gain,
    video_gain,
    w_query,
    w_key,
    w_value,
    w_text_key,
    w_text_value,
    w_out,
):
    smem = pl.BlockSpec(memory_space=pltpu.SMEM)
    vmem = pl.BlockSpec(memory_space=pltpu.VMEM)
    hbm = pl.BlockSpec(memory_space=pl.ANY)
    dma = pltpu.SemaphoreType.DMA
    width, half, quarter = 4096, 2048, 1024
    return pl.pallas_call(
        kernel,
        out_shape=jax.ShapeDtypeStruct(video.shape, video.dtype),
        in_specs=[smem] * 3 + [vmem] * 5 + [hbm] * 9,
        out_specs=vmem,
        scratch_shapes=[
            pltpu.VMEM((6, 16, 256, 256), BF),
            pltpu.VMEM((16, 8, width), BF),
            pltpu.VMEM((8, width), BF),
            pltpu.VMEM((16, 8, width), BF),
            pltpu.VMEM((128, width), BF),
            pltpu.VMEM(ffn_gate.shape, BF),
            pltpu.VMEM(ffn_up.shape, BF),
            pltpu.VMEM(ffn_down.shape, BF),
            pltpu.VMEM((128, 384), F32),
            pltpu.VMEM((128, 384), F32),
            pltpu.VMEM((128, 384), BF),
            pltpu.VMEM((8, 2, 8, width), BF),
            pltpu.VMEM((8, 8, width), BF),
            pltpu.VMEM((8, 8, width), BF),
            pltpu.VMEM((8, 8, width), BF),
            pltpu.VMEM((8, width), BF),
            pltpu.VMEM((16, 8, width), BF),
            pltpu.VMEM((2, 32, half), BF),
            pltpu.VMEM((2, 4, 2, 2, 32, half), BF),
            pltpu.VMEM((512, 256), F32),
            pltpu.VMEM((512, 256), F32),
            pltpu.VMEM((512, 256), F32),
            pltpu.VMEM((512, 256), BF),
            pltpu.VMEM((4, 2, 128, 640), BF),
            pltpu.VMEM((640, 256), BF),
            pltpu.VMEM((640, 256), BF),
            pltpu.VMEM((4, 4, 128, 256), BF),
            pltpu.VMEM((4, 4, 256, 256), BF),
            pltpu.VMEM((16, 32, quarter), BF),
            pltpu.VMEM((3, 8, 32, quarter), BF),
            pltpu.VMEM((8, 32, quarter), BF),
            pltpu.VMEM((4, 32, quarter), BF),
            pltpu.VMEM((8, 128), jnp.int32),
            pltpu.VMEM((8, 128), jnp.int32),
            dma((3,)),
            dma((7, 8)),
            dma((7,)),
            dma((8,)),
            dma((7,)),
            dma,
            dma((3,)),
            dma((3,)),
            dma((3,)),
            dma((6,)),
            dma((4,)),
            dma((5,)),
            dma((9,)),
            dma((5,)),
            dma((4,)),
            dma,
        ],
        compiler_params=pltpu.CompilerParams(
            collective_id=0, has_side_effects=True, vmem_limit_bytes=58 * 1024 * 1024
        ),
        name="joint_attention",
    )(
        video_length,
        prompt_length,
        prompt_choice,
        video,
        prompt,
        ffn_gain.reshape(1, -1),
        final_gain.reshape(1, -1),
        video_gain.reshape(1, -1),
        ffn_gate,
        ffn_up,
        ffn_down,
        w_text_key,
        w_text_value,
        w_query,
        w_key,
        w_value,
        w_out,
    )


def solution(mesh):
    in_specs = (
        P("vid", "seq", None),
        P("vid"),
        P("vid", "seq", None),
        P(),
        P("vid"),
        P(),
        P(None, "seq"),
        P(None, "seq"),
        P("seq", None),
        P(),
        P(),
        P("vid", "seq"),
        P("vid", "seq"),
        P("vid", "seq"),
        P("vid", "seq"),
        P("vid", "seq"),
        P("seq", "vid"),
    )
    out_specs = P("vid", "seq", None)
    return jax.shard_map(block, mesh=mesh, in_specs=in_specs, out_specs=out_specs, check_vma=False)
```

```python
import jax
import jax.numpy as jnp
from jax import lax
from jax.experimental import pallas as pl
from jax.experimental.pallas import tpu as pltpu
from jax.sharding import PartitionSpec as P

HD = 128
EPSILON = 1e-06
MESH = pl.DeviceIdType.MESH
BF = jnp.bfloat16
F32 = jnp.float32

TK, TV, Q, K, V, O, PROMPT = range(7)


def rms_norm(values, gain):
    return values * lax.rsqrt(jnp.mean(values * values, axis=-1, keepdims=True) + EPSILON) * gain


def kernel(
    length_ref,
    prompt_length_ref,
    choice_ref,
    video_ref,
    prompt_ref,
    ffn_gain_ref,
    final_gain_ref,
    video_gain_ref,
    gate_hbm,
    up_hbm,
    down_hbm,
    w_text_key,
    w_text_value,
    w_query,
    w_key,
    w_value,
    w_out,
    out_ref,
    W,
    PB,
    SEL,
    PG,
    FN,
    gate_ref,
    up_ref,
    down_ref,
    gate_acc,
    up_acc,
    hidden,
    FP,
    FS,
    FQ,
    FR,
    TX,
    TG,
    NV,
    XG,
    q_acc,
    k_acc,
    v_acc,
    queries,
    probs,
    keys,
    values,
    AX,
    OX,
    SB,
    YR,
    YS,
    RR,
    info_own,
    info,
    ffn_sem,
    ring_recv,
    ring_send,
    swap_send,
    sib_recv,
    info_sem,
    group_recv,
    group_send,
    group_send0,
    prompt_sem,
    video_recv,
    video_send,
    out_recv,
    out_send,
):
    vid, seq = lax.axis_index("vid"), lax.axis_index("seq")
    yh, z = vid // 8, vid % 8
    x, yl, c = seq // 4, (seq // 2) % 2, seq % 2
    y = yh * 2 + yl
    diag = c == yh
    taken = (y + 3) % 4
    head_block = x * 4 + (taken % 2) * 2 + taken // 2
    taker = (yl + 1 + 2 * c) % 4
    taker = ((taker // 2) * 8 + z, x * 4 + (taker % 2) * 2 + yh)
    sibling = (vid, seq + 1 - 2 * c)
    z_right = (yh * 8 + (z + 1) % 8, seq)
    z_left = (yh * 8 + (z + 7) % 8, seq)

    def to_chip(k):
        xk, yk = (x + k // 4) % 4, (y + k % 4) % 4
        return ((yk // 2) * 8 + z, xk * 4 + (yk % 2) * 2 + yh)

    def place(k):
        return ((x + k // 4) % 4) * 4 + ((yl + (k // 2) % 2) % 2) * 2 + (c + k % 2) % 2

    def local(src, dst, sem):
        return pltpu.make_async_copy(src, dst, sem)

    def remote(src, dst, send, recv, device):
        return pltpu.make_async_remote_copy(
            src_ref=src, dst_ref=dst, send_sem=send, recv_sem=recv, device_id=device, device_id_type=MESH
        )

    ffn_copies = [
        local(gate_hbm, gate_ref, ffn_sem.at[0]),
        local(up_hbm, up_ref, ffn_sem.at[1]),
        local(down_hbm, down_ref, ffn_sem.at[2]),
    ]
    for copy in ffn_copies:
        copy.start()

    barrier = pltpu.get_barrier_semaphore()

    def greet(k, carry):
        seq_k = (seq + k) % 16
        vid_k = ((yh + k // 16) % 2) * 8 + z
        pl.semaphore_signal(barrier, inc=1, device_id=(vid_k, seq_k), device_id_type=MESH)
        return carry

    lax.fori_loop(1, 32, greet, 0)
    for neighbour in (z_left, z_right):
        pl.semaphore_signal(barrier, inc=1, device_id=neighbour, device_id_type=MESH)

    choice = choice_ref[0]
    row = lax.broadcasted_iota(jnp.int32, (8, 128), 0)
    text_live = prompt_length_ref[choice]
    info_own[...] = jnp.where(row == 0, choice, jnp.where(row == 1, length_ref[0], text_live))

    normed = rms_norm(video_ref[0].astype(F32), video_gain_ref[...]).astype(BF)
    NV[0] = normed[:, :2048]
    NV[1] = normed[:, 2048:]

    pl.semaphore_wait(barrier, 33)

    sources = [w_text_key, w_text_value, w_query, w_key, w_value, w_out, prompt_ref.at[0]]

    def slot(w, block):
        return PB.at[block] if w == PROMPT else OX.at[block] if w == O else W.at[w, block]

    def swap_copy(w):
        return remote(sources[w], slot(w, yh * 8 + z), swap_send.at[w], ring_recv.at[w, z], taker)

    info_copy = remote(info_own, info, swap_send.at[7], info_sem, taker)
    swap_copy(PROMPT).start()
    info_copy.start()

    def swap_half(half):
        taker_y = (yl + 1 + 2 * c) % 4
        device = ((taker_y // 2) * 8 + z, (2 * yh + half) * 4 + (taker_y % 2) * 2 + x // 2)
        return remote(
            w_out.at[:, pl.ds(half * 128, 128)],
            OX.at[(x // 2) * 8 + z, x % 2],
            swap_send.at[O],
            ring_recv.at[O, z],
            device,
        )

    def swap(w):
        if w == O:
            swap_half(0).start()
            swap_half(1).start()
        else:
            swap_copy(w).start()

    def ring_wait(w, zz):
        ref = slot(w, c * 8 + zz)
        local(ref, ref, ring_recv.at[w, zz]).wait()

    def ring_to(w, zz, device):
        ref = slot(w, c * 8 + zz)
        remote(ref, ref, ring_send.at[w], ring_recv.at[w, zz], device).start()

    def to_sibling(w, zz):
        if w == PROMPT:
            return
        ref = slot(w, c * 8 + zz)
        remote(ref, ref, ring_send.at[w], sib_recv.at[w], sibling).start()

    def own(w):
        ring_wait(w, z)
        ring_to(w, z, z_right)
        ring_to(w, z, z_left)
        to_sibling(w, z)

    def hop(w, k):
        right_hops = 4 if w % 2 == 0 else 3
        left_hops = 7 - right_hops
        from_left, from_right = (z + 8 - k) % 8, (z + k) % 8
        if k <= right_hops:
            ring_wait(w, from_left)
            if k < right_hops:
                ring_to(w, from_left, z_right)
        if k <= left_hops:
            ring_wait(w, from_right)
            if k < left_hops:
                ring_to(w, from_right, z_left)
        if k <= right_hops:
            to_sibling(w, from_left)
        if k <= left_hops:
            to_sibling(w, from_right)

    def sibling_wait(w):
        ref = OX.at[pl.ds(0, 8)] if w == O else W.at[w, pl.ds(0, 8)]
        local(ref, ref, sib_recv.at[w]).wait()

    not_diag = jnp.logical_not(diag)

    def at_core(xk, yk, core):
        return ((yk // 2) * 8 + z, xk * 4 + (yk % 2) * 2 + core)

    def video_slot(h):
        return XG.at[h, x, yl, c]

    def video_x(k):
        return remote(
            NV.at[0], video_slot(0), video_send.at[0], video_recv.at[0], at_core((x + k) % 4, y, yh)
        )

    def video_y(k):
        return remote(
            NV.at[1], video_slot(1), video_send.at[1], video_recv.at[1], at_core(x, (y + k) % 4, yh)
        )

    own_chip = [
        remote(
            NV.at[h], video_slot(h), video_send.at[4], video_recv.at[h], sibling
        )
        for h in range(2)
    ]

    def keep_video(h):
        @pl.when(diag)
        def _():
            local(NV.at[h], video_slot(h), video_recv.at[h]).start()

        @pl.when(not_diag)
        def _():
            own_chip[h].start()

    def send_lower():
        keep_video(0)
        for k in (2, 1, 3):
            video_x(k).start()

    def send_upper():
        keep_video(1)
        for k in (2, 1, 3):
            video_y(k).start()

    def lower_on(k):
        ref = XG.at[0, :, yl]
        return remote(ref, ref, video_send.at[2], video_recv.at[2], at_core(x, (y + k) % 4, c))

    def upper_on(k):
        ref = XG.at[1, x]
        return remote(ref, ref, video_send.at[3], video_recv.at[3], at_core((x + k) % 4, y, c))

    def pass_upper_on():
        ref = XG.at[1, 0]
        local(ref, ref, video_recv.at[1]).wait()
        for k in (2, 1, 3):
            upper_on(k).start()

    def pass_lower_on():
        @pl.when(diag)
        def _():
            ref = XG.at[0, pl.ds(0, 2)]
            local(ref, ref, video_recv.at[0]).wait()
            for k in (2, 1, 3):
                lower_on(k).start()

    def video_wait():
        ref = XG.at[1, pl.ds(0, 3)]
        local(ref, ref, video_recv.at[3]).wait()

        @pl.when(diag)
        def _():
            ref = XG.at[0, pl.ds(0, 2)]
            local(ref, ref, video_recv.at[2]).wait()

        @pl.when(not_diag)
        def _():
            ref = XG.at[0]
            local(ref, ref, video_recv.at[2]).wait()

    PROMPTS, SUMS, TEXT = range(3)

    def send_prompt(k):
        device = (c * 8 + z, ((x + k // 2) % 4) * 4 + ((yl + k % 2) % 2) * 2 + x // 2)
        return remote(SEL, PG.at[head_block], group_send.at[PROMPTS], group_recv.at[PROMPTS], device)

    half_chosen = PG.at[pl.ds(pl.multiple_of(c * 8, 8), 8)]
    pass_chosen = remote(half_chosen, half_chosen, prompt_sem.at[2], prompt_sem.at[3], sibling)

    def pass_chosen_on():
        local(half_chosen, half_chosen, group_recv.at[PROMPTS]).wait()
        pass_chosen.start()

    def spread(first, last, make):
        def step(k, carry):
            make(k).start()
            return carry

        lax.fori_loop(first, last, step, 0)

    def first_send(copy, copy_local, group):
        @pl.when(diag)
        def _():
            copy_local.start()

        @pl.when(jnp.logical_not(diag))
        def _():
            copy.start()

    prompt0 = remote(
        SEL,
        PG.at[head_block],
        group_send0.at[PROMPTS],
        group_recv.at[PROMPTS],
        (c * 8 + z, x * 4 + yl * 2 + x // 2),
    )
    chosen_here = jnp.logical_and(diag, c == x // 2)

    def send_prompts():
        ring_wait(PROMPT, z)
        ref = PB.at[c * 8 + z]

        def step(k, carry):
            remote(
                ref, ref, ring_send.at[PROMPT], sib_recv.at[PROMPT], (yh * 8 + (z + k) % 8, seq)
            ).start()
            return carry

        lax.fori_loop(1, 8, step, 0)

    half_prompts = PB.at[pl.ds(pl.multiple_of(c * 8, 8), 8)]
    pass_prompts = remote(half_prompts, half_prompts, prompt_sem.at[0], prompt_sem.at[1], sibling)

    def pass_prompts_on():
        ref = PB.at[pl.ds(0, 7)]
        local(ref, ref, sib_recv.at[PROMPT]).wait()
        pass_prompts.start()

    def choose_prompt():
        pass_prompts.wait_recv()
        local(info, info, info_sem).wait()
        wanted = info[0:1, 0:1]

        def pick(i, total):
            return total + jnp.where(wanted == i, PB[i].astype(F32), 0.0)

        SEL[...] = lax.fori_loop(0, 16, pick, jnp.zeros(SEL.shape, F32)).astype(BF)

        @pl.when(chosen_here)
        def _():
            local(SEL, PG.at[head_block], group_recv.at[PROMPTS]).start()

        @pl.when(jnp.logical_not(chosen_here))
        def _():
            prompt0.start()

        spread(1, 8, send_prompt)

    def norm_rows(i, carry):
        rows = PG[pl.ds(2 * i, 2)].astype(F32).reshape(16, PG.shape[2])
        FN[pl.ds(pl.multiple_of(i * 16, 16), 16), :] = rms_norm(rows, ffn_gain_ref[...]).astype(BF)
        return carry

    def ffn_norm():
        pass_chosen.wait_recv()
        lax.fori_loop(0, 8, norm_rows, 0)

    def ffn_project(weights, acc, copy):
        copy.wait()

        def step(i, total):
            at = pl.ds(pl.multiple_of(i * 512, 512), 512)
            return total + jnp.dot(FN[:, at], weights[at, :], preferred_element_type=F32)

        acc[...] = lax.fori_loop(0, 8, step, jnp.zeros(acc.shape, F32))

    def ffn_gate():
        ffn_project(gate_ref, gate_acc, ffn_copies[0])

    def ffn_up():
        ffn_project(up_ref, up_acc, ffn_copies[1])
        hidden[...] = (jax.nn.gelu(gate_acc[...], approximate=True) * up_acc[...]).astype(BF)

    def down_proj(i, carry):
        at = pl.ds(pl.multiple_of(i * 256, 256), 256)
        part = jnp.dot(hidden[...], down_ref[:, at], preferred_element_type=F32)
        FP[:, :, :, at] = part.reshape(8, 2, 8, 256).astype(BF)
        return carry

    pass_sums = remote(FP.at[:, 1 - c], FS, prompt_sem.at[4], prompt_sem.at[5], sibling)
    own_chip_index = seq // 2

    def send_sums(k):
        to = ((x + k // 2) % 4) * 2 + (yl + k % 2) % 2
        return remote(
            FQ.at[to], FR.at[own_chip_index], group_send.at[SUMS], group_recv.at[SUMS], (vid, to * 2 + c)
        )

    def ffn_down():
        ffn_copies[2].wait()
        lax.fori_loop(0, 16, down_proj, 0)
        pass_sums.start()

    def ffn_sums():
        pass_sums.wait_recv()

        def step(i, carry):
            FQ[i] = (FP[i, c].astype(F32) + FS[i].astype(F32)).astype(BF)
            return carry

        lax.fori_loop(0, 8, step, 0)
        local(FQ.at[own_chip_index], FR.at[own_chip_index], group_recv.at[SUMS]).start()
        spread(1, 8, send_sums)

    def send_text(k):
        return remote(TX, TG.at[seq], group_send.at[TEXT], group_recv.at[TEXT], to_chip(k))

    text0 = remote(TX, TG.at[seq], group_send0.at[TEXT], group_recv.at[TEXT], to_chip(0))

    def text_rows():
        local(FR, FR, group_recv.at[SUMS]).wait()
        encoded = lax.fori_loop(
            0, 8, lambda i, total: total + FR[i].astype(F32), jnp.zeros(TX.shape, F32)
        )
        encoded = PG[seq].astype(F32) + encoded
        TX[...] = rms_norm(encoded, final_gain_ref[...]).astype(BF)
        first_send(text0, local(TX, TG.at[seq], group_recv.at[TEXT]), TEXT)
        spread(1, 16, send_text)

    def video_rows(j):
        at = pl.ds(pl.multiple_of((j % 4) * 512, 512), 512)
        return XG[j // 4, :, :, :, :, at].reshape(512, 512)

    def project(w, acc, result):
        sibling_wait(w)
        acc[...] = jnp.zeros_like(acc)

        def step(j, carry):
            weights = W[w, pl.ds(2 * j, 2)].reshape(512, 256)
            acc[...] += jnp.dot(video_rows(j), weights, preferred_element_type=F32)
            return carry

        lax.fori_loop(0, 8, step, 0)
        result[pl.ds(0, 512), :] = acc[...].astype(BF)

    def text_key_value(j, carry):
        at = pl.ds(pl.multiple_of(j * 256, 256), 256)
        rows = TG[:, :, at].astype(F32).reshape(128, 256).astype(BF)
        key_sum, value_sum = carry
        key_sum = key_sum + jnp.dot(rows, W[TK, j], preferred_element_type=F32)
        value_sum = value_sum + jnp.dot(rows, W[TV, j], preferred_element_type=F32)
        return key_sum, value_sum

    def text_projections():
        local(TG, TG, group_recv.at[TEXT]).wait()
        sibling_wait(TK)
        sibling_wait(TV)
        zero = jnp.zeros((128, 256), F32)
        text_key, text_value = lax.fori_loop(0, 16, text_key_value, (zero, zero))
        keys[pl.ds(512, 128), :] = text_key.astype(BF)
        values[pl.ds(512, 128), :] = text_value.astype(BF)

    def attended_x(part, xk):
        ref = AX.at[x, part]
        return remote(ref, ref, out_send.at[0], out_recv.at[part], at_core(xk, y, c))

    def out_y(part, k):
        return remote(
            SB.at[pl.ds(part * 4 + k * 2, 2)],
            YR.at[(y + 3 - (c * 2 + k)) % 4, pl.ds(part * 2, 2)],
            out_send.at[1 + k],
            out_recv.at[4 + part],
            at_core(x, c * 2 + k, c),
        )

    def sum_y(xk, core):
        return remote(
            YS.at[xk * 2 + core], RR.at[x], out_send.at[3], out_recv.at[8], at_core(xk, y, core)
        )

    def attention_probs(first, last):
        position = lax.broadcasted_iota(jnp.int32, (1, 640), 1)
        live = position < jnp.where(position < 512, info[1:2, 0:1], info[2:3, 0:1] + 512)

        def step(i, carry):
            part = (x + 1 + i) % 4
            rows = pl.ds(pl.multiple_of(part * 128, 128), 128)
            for h in range(2):
                lanes = pl.ds(h * HD, HD)
                scores = lax.dot_general(
                    queries[rows, lanes], keys[:, lanes], (((1,), (1,)), ((), ())), preferred_element_type=F32
                )
                scores = jnp.where(live, scores * HD ** (-0.5), -1e30)
                e = jnp.exp(scores - jnp.max(scores, axis=-1, keepdims=True))
                probs[part, h] = (e / jnp.sum(e, axis=-1, keepdims=True)).astype(BF)
            return carry

        lax.fori_loop(first, last, step, 0)

    def attend(part, carry):
        for h in range(2):
            lanes = pl.ds(h * HD, HD)
            AX[x, part, :, lanes] = jnp.dot(
                probs[part, h], values[:, lanes], preferred_element_type=F32
            ).astype(BF)
        return carry

    def attend_all():
        lax.fori_loop(0, 4, attend, 0)

        def step(i, carry):
            for k in (2, 1, 3):
                xk = (x + k) % 4
                attended_x((xk + 1 + i) % 4, xk).start()
            return carry

        lax.fori_loop(0, 4, step, 0)

    def project_part(i, carry):
        part = (x + 1 + i) % 4
        ref = AX.at[pl.ds(0, 3), 0]
        local(ref, ref, out_recv.at[part]).wait()
        rows = [jnp.concatenate([AX[2 * j, part], AX[2 * j + 1, part]], axis=1) for j in range(2)]
        for m in range(4):
            total = jnp.zeros((128, 256), F32)
            for j in range(2):
                weights = jnp.concatenate(
                    [OX[j * 8 + 2 * m + i].reshape(512, 128) for i in range(2)], axis=1
                )
                total = total + jnp.dot(rows[j], weights, preferred_element_type=F32)
            SB[pl.ds(part * 4, 4), :, pl.ds(m * 256, 256)] = total.reshape(4, 32, 256).astype(BF)
        for k in range(2):

            @pl.when(y != c * 2 + k)
            def _():
                out_y(part, k).start()

        return carry

    def sum_part(i, carry):
        part = (x + 1 + i) % 4
        ref = YR.at[pl.ds(0, 3), pl.ds(0, 2)]
        local(ref, ref, out_recv.at[4 + part]).wait()
        for step in range(2):
            core = (c + 1 + step) % 2
            total = SB[part * 4 + yl * 2 + core].astype(F32)
            for j in range(3):
                total = total + YR[j, part * 2 + core].astype(F32)
            YS[part * 2 + core] = total.astype(BF)
            to_here = jnp.logical_and(part == x, core == c)

            @pl.when(jnp.logical_not(to_here))
            def _():
                sum_y(part, core).start()

            @pl.when(to_here)
            def _():
                local(YS.at[part * 2 + core], RR.at[x], out_recv.at[8]).start()

        return carry

    send_lower()
    swap(TK)
    own(PROMPT)
    swap(TV)
    hop(PROMPT, 1)
    send_upper()
    swap(Q)
    own(TK)
    hop(PROMPT, 2)
    own(TV)
    swap(K)
    hop(PROMPT, 3)
    own(Q)
    swap(O)
    hop(PROMPT, 4)
    pass_prompts.start()
    swap(V)
    own(K)
    hop(TK, 1)
    choose_prompt()
    hop(TV, 1)
    hop(Q, 1)
    hop(K, 1)
    own(O)
    own(V)
    pass_chosen_on()
    pass_upper_on()
    pass_lower_on()
    ffn_norm()
    ffn_gate()
    ffn_up()
    hop(TK, 2)
    hop(TV, 2)
    hop(Q, 2)
    hop(K, 2)
    hop(O, 1)
    ffn_down()
    hop(V, 1)
    hop(TK, 3)
    ffn_sums()
    hop(TV, 3)
    hop(Q, 3)
    hop(K, 3)
    hop(O, 2)
    hop(V, 2)
    text_rows()
    hop(TK, 4)
    hop(TV, 4)
    hop(Q, 4)
    hop(K, 4)
    video_wait()
    project(Q, q_acc, queries)
    hop(O, 3)
    hop(V, 3)
    project(K, k_acc, keys)
    hop(V, 4)
    text_projections()
    attention_probs(0, 4)
    project(V, v_acc, values)
    hop(O, 4)
    attend_all()
    sibling_wait(O)
    lax.fori_loop(0, 4, project_part, 0)

    @pl.when(diag)
    def _():
        lax.fori_loop(0, 4, sum_part, 0)

    local(RR, RR, out_recv.at[8]).wait()
    row_position = seq * 32 + lax.broadcasted_iota(jnp.int32, (32, 1), 0)
    row_live = row_position < length_ref[0]

    for j in range(4):
        for i in range(8):
            at = pl.ds((j // 2) * 2048 + i * 256 + (j % 2) * 128, 128)
            total = RR[j, :, pl.ds(i * 128, 128)].astype(F32)
            updated = video_ref[0, :, at].astype(F32) + jnp.where(row_live, total, 0.0)
            out_ref[0, :, at] = updated.astype(BF)

    for w in (TK, TV, Q, K, V, PROMPT):
        swap_copy(w).wait_send()
    local(OX.at[0], OX.at[0], swap_send.at[O]).wait()
    info_copy.wait_send()

    @pl.when(jnp.logical_not(diag))
    def _():
        text0.wait_send()
        both = XG.at[0, 0, 0]
        local(both, both, video_send.at[4]).wait()

    pass_prompts.wait_send()
    for w in range(7):
        ref = slot(w, pl.ds(0, 7 if w == PROMPT else 15))
        local(ref, ref, ring_send.at[w]).wait()
    @pl.when(jnp.logical_not(chosen_here))
    def _():
        prompt0.wait_send()

    pass_chosen.wait_send()
    pass_sums.wait_send()
    for group, buffer in ((PROMPTS, PG), (SUMS, FR), (TEXT, TG)):
        ref = buffer.at[pl.ds(0, 15 if group == TEXT else 7)]
        local(ref, ref, group_send.at[group]).wait()
    for sem in (video_send.at[0], video_send.at[1]):
        ref = XG.at[0, pl.ds(0, 3), 0, 0]
        local(ref, ref, sem).wait()
    ref = XG.at[0, pl.ds(0, 3)]
    local(ref, ref, video_send.at[3]).wait()
    ref = AX.at[pl.ds(0, 3)]
    local(ref, ref, out_send.at[0]).wait()
    for k in range(2):

        @pl.when(y != c * 2 + k)
        def _():
            ref = SB.at[pl.ds(0, 8)]
            local(ref, ref, out_send.at[1 + k]).wait()

    @pl.when(diag)
    def _():
        ref = XG.at[:, pl.ds(0, 3)]
        local(ref, ref, video_send.at[2]).wait()
        ref = YS.at[pl.ds(0, 7)]
        local(ref, ref, out_send.at[3]).wait()


def block(
    video,
    video_length,
    prompt,
    prompt_length,
    prompt_choice,
    ffn_gain,
    ffn_gate,
    ffn_up,
    ffn_down,
    final_gain,
    video_gain,
    w_query,
    w_key,
    w_value,
    w_text_key,
    w_text_value,
    w_out,
):
    smem = pl.BlockSpec(memory_space=pltpu.SMEM)
    vmem = pl.BlockSpec(memory_space=pltpu.VMEM)
    hbm = pl.BlockSpec(memory_space=pl.ANY)
    dma = pltpu.SemaphoreType.DMA
    width, half, quarter = 4096, 2048, 1024
    return pl.pallas_call(
        kernel,
        out_shape=jax.ShapeDtypeStruct(video.shape, video.dtype),
        in_specs=[smem] * 3 + [vmem] * 5 + [hbm] * 9,
        out_specs=vmem,
        scratch_shapes=[
            pltpu.VMEM((5, 16, 256, 256), BF),
            pltpu.VMEM((16, 8, width), BF),
            pltpu.VMEM((8, width), BF),
            pltpu.VMEM((16, 8, width), BF),
            pltpu.VMEM((128, width), BF),
            pltpu.VMEM(ffn_gate.shape, BF),
            pltpu.VMEM(ffn_up.shape, BF),
            pltpu.VMEM(ffn_down.shape, BF),
            pltpu.VMEM((128, 384), F32),
            pltpu.VMEM((128, 384), F32),
            pltpu.VMEM((128, 384), BF),
            pltpu.VMEM((8, 2, 8, width), BF),
            pltpu.VMEM((8, 8, width), BF),
            pltpu.VMEM((8, 8, width), BF),
            pltpu.VMEM((8, 8, width), BF),
            pltpu.VMEM((8, width), BF),
            pltpu.VMEM((16, 8, width), BF),
            pltpu.VMEM((2, 32, half), BF),
            pltpu.VMEM((2, 4, 2, 2, 32, half), BF),
            pltpu.VMEM((512, 256), F32),
            pltpu.VMEM((512, 256), F32),
            pltpu.VMEM((512, 256), F32),
            pltpu.VMEM((512, 256), BF),
            pltpu.VMEM((4, 2, 128, 640), BF),
            pltpu.VMEM((640, 256), BF),
            pltpu.VMEM((640, 256), BF),
            pltpu.VMEM((4, 4, 128, 256), BF),
            pltpu.VMEM((16, 2, 256, 128), BF),
            pltpu.VMEM((16, 32, quarter), BF),
            pltpu.VMEM((3, 8, 32, quarter), BF),
            pltpu.VMEM((8, 32, quarter), BF),
            pltpu.VMEM((4, 32, quarter), BF),
            pltpu.VMEM((8, 128), jnp.int32),
            pltpu.VMEM((8, 128), jnp.int32),
            dma((3,)),
            dma((7, 8)),
            dma((7,)),
            dma((8,)),
            dma((7,)),
            dma,
            dma((3,)),
            dma((3,)),
            dma((3,)),
            dma((6,)),
            dma((4,)),
            dma((5,)),
            dma((9,)),
            dma((5,)),
        ],
        compiler_params=pltpu.CompilerParams(
            collective_id=0, has_side_effects=True, vmem_limit_bytes=58 * 1024 * 1024
        ),
        name="joint_attention",
    )(
        video_length,
        prompt_length,
        prompt_choice,
        video,
        prompt,
        ffn_gain.reshape(1, -1),
        final_gain.reshape(1, -1),
        video_gain.reshape(1, -1),
        ffn_gate,
        ffn_up,
        ffn_down,
        w_text_key,
        w_text_value,
        w_query,
        w_key,
        w_value,
        w_out,
    )


def solution(mesh):
    in_specs = (
        P("vid", "seq", None),
        P("vid"),
        P("vid", "seq", None),
        P(),
        P("vid"),
        P(),
        P(None, "seq"),
        P(None, "seq"),
        P("seq", None),
        P(),
        P(),
        P("vid", "seq"),
        P("vid", "seq"),
        P("vid", "seq"),
        P("vid", "seq"),
        P("vid", "seq"),
        P("seq", "vid"),
    )
    out_specs = P("vid", "seq", None)
    return jax.shard_map(block, mesh=mesh, in_specs=in_specs, out_specs=out_specs, check_vma=False)
```

```python
import jax
import jax.numpy as jnp
from jax import lax
from jax.experimental import pallas as pl
from jax.experimental.pallas import tpu as pltpu
from jax.sharding import PartitionSpec as P

HD = 128
EPSILON = 1e-06
MESH = pl.DeviceIdType.MESH
BF = jnp.bfloat16
F32 = jnp.float32

TK, TV, Q, K, V, O, PROMPT = range(7)


def rms_norm(values, gain):
    return values * lax.rsqrt(jnp.mean(values * values, axis=-1, keepdims=True) + EPSILON) * gain


def kernel(
    length_ref,
    prompt_length_ref,
    choice_ref,
    video_ref,
    prompt_ref,
    ffn_gain_ref,
    final_gain_ref,
    video_gain_ref,
    gate_hbm,
    up_hbm,
    down_hbm,
    w_text_key,
    w_text_value,
    w_query,
    w_key,
    w_value,
    w_out,
    out_ref,
    W,
    PB,
    SEL,
    PG,
    FN,
    gate_ref,
    up_ref,
    down_ref,
    gate_acc,
    up_acc,
    hidden,
    FP,
    FS,
    FQ,
    FR,
    TX,
    TG,
    NV,
    XG,
    q_acc,
    k_acc,
    v_acc,
    queries,
    probs,
    keys,
    values,
    AX,
    OX,
    SB,
    YR,
    YS,
    RR,
    info_own,
    info,
    ffn_sem,
    ring_recv,
    ring_send,
    swap_send,
    sib_recv,
    info_sem,
    group_recv,
    group_send,
    group_send0,
    prompt_sem,
    video_recv,
    video_send,
    out_recv,
    out_send,
):
    vid, seq = lax.axis_index("vid"), lax.axis_index("seq")
    yh, z = vid // 8, vid % 8
    x, yl, c = seq // 4, (seq // 2) % 2, seq % 2
    y = yh * 2 + yl
    diag = c == yh
    taken = (y + 3) % 4
    head_block = x * 4 + (taken % 2) * 2 + taken // 2
    taker = (yl + 1 + 2 * c) % 4
    taker = ((taker // 2) * 8 + z, x * 4 + (taker % 2) * 2 + yh)
    sibling = (vid, seq + 1 - 2 * c)
    z_right = (yh * 8 + (z + 1) % 8, seq)
    z_left = (yh * 8 + (z + 7) % 8, seq)

    def to_chip(k):
        xk, yk = (x + k // 4) % 4, (y + k % 4) % 4
        return ((yk // 2) * 8 + z, xk * 4 + (yk % 2) * 2 + yh)

    def place(k):
        return ((x + k // 4) % 4) * 4 + ((yl + (k // 2) % 2) % 2) * 2 + (c + k % 2) % 2

    def local(src, dst, sem):
        return pltpu.make_async_copy(src, dst, sem)

    def remote(src, dst, send, recv, device):
        return pltpu.make_async_remote_copy(
            src_ref=src, dst_ref=dst, send_sem=send, recv_sem=recv, device_id=device, device_id_type=MESH
        )

    ffn_copies = [
        local(gate_hbm, gate_ref, ffn_sem.at[0]),
        local(up_hbm, up_ref, ffn_sem.at[1]),
        local(down_hbm, down_ref, ffn_sem.at[2]),
    ]
    for copy in ffn_copies:
        copy.start()

    barrier = pltpu.get_barrier_semaphore()

    def greet(k, carry):
        seq_k = (seq + k) % 16
        vid_k = ((yh + k // 16) % 2) * 8 + z
        pl.semaphore_signal(barrier, inc=1, device_id=(vid_k, seq_k), device_id_type=MESH)
        return carry

    lax.fori_loop(1, 32, greet, 0)
    for neighbour in (z_left, z_right):
        pl.semaphore_signal(barrier, inc=1, device_id=neighbour, device_id_type=MESH)

    choice = choice_ref[0]
    row = lax.broadcasted_iota(jnp.int32, (8, 128), 0)
    text_live = prompt_length_ref[choice]
    info_own[...] = jnp.where(row == 0, choice, jnp.where(row == 1, length_ref[0], text_live))

    normed = rms_norm(video_ref[0].astype(F32), video_gain_ref[...]).astype(BF)
    NV[0] = normed[:, :2048]
    NV[1] = normed[:, 2048:]

    pl.semaphore_wait(barrier, 33)

    sources = [w_text_key, w_text_value, w_query, w_key, w_value, w_out, prompt_ref.at[0]]

    def slot(w, block):
        return PB.at[block] if w == PROMPT else OX.at[block] if w == O else W.at[w, block]

    def swap_copy(w):
        return remote(sources[w], slot(w, yh * 8 + z), swap_send.at[w], ring_recv.at[w, z], taker)

    info_copy = remote(info_own, info, swap_send.at[7], info_sem, taker)
    swap_copy(PROMPT).start()
    info_copy.start()

    def swap_half(half):
        taker_y = (yl + 1 + 2 * c) % 4
        device = ((taker_y // 2) * 8 + z, (2 * yh + half) * 4 + (taker_y % 2) * 2 + x // 2)
        return remote(
            w_out.at[:, pl.ds(half * 128, 128)],
            OX.at[(x // 2) * 8 + z, x % 2],
            swap_send.at[O],
            ring_recv.at[O, z],
            device,
        )

    def swap(w):
        if w == O:
            swap_half(0).start()
            swap_half(1).start()
        else:
            swap_copy(w).start()

    def ring_wait(w, zz):
        ref = slot(w, c * 8 + zz)
        local(ref, ref, ring_recv.at[w, zz]).wait()

    def ring_to(w, zz, device):
        ref = slot(w, c * 8 + zz)
        remote(ref, ref, ring_send.at[w], ring_recv.at[w, zz], device).start()

    def to_sibling(w, zz):
        if w == PROMPT:
            return
        ref = slot(w, c * 8 + zz)
        remote(ref, ref, ring_send.at[w], sib_recv.at[w], sibling).start()

    def own(w):
        ring_wait(w, z)
        ring_to(w, z, z_right)
        ring_to(w, z, z_left)
        to_sibling(w, z)

    def hop(w, k):
        right_hops = 4 if w % 2 == 0 else 3
        left_hops = 7 - right_hops
        from_left, from_right = (z + 8 - k) % 8, (z + k) % 8
        if k <= right_hops:
            ring_wait(w, from_left)
            if k < right_hops:
                ring_to(w, from_left, z_right)
        if k <= left_hops:
            ring_wait(w, from_right)
            if k < left_hops:
                ring_to(w, from_right, z_left)
        if k <= right_hops:
            to_sibling(w, from_left)
        if k <= left_hops:
            to_sibling(w, from_right)

    def sibling_wait(w):
        ref = OX.at[pl.ds(0, 8)] if w == O else W.at[w, pl.ds(0, 8)]
        local(ref, ref, sib_recv.at[w]).wait()

    not_diag = jnp.logical_not(diag)

    def at_core(xk, yk, core):
        return ((yk // 2) * 8 + z, xk * 4 + (yk % 2) * 2 + core)

    def video_slot(h):
        return XG.at[h, x, yl, c]

    def video_x(k):
        return remote(
            NV.at[0], video_slot(0), video_send.at[0], video_recv.at[0], at_core((x + k) % 4, y, yh)
        )

    def video_y(k):
        return remote(
            NV.at[1], video_slot(1), video_send.at[1], video_recv.at[1], at_core(x, (y + k) % 4, yh)
        )

    own_chip = [
        remote(
            NV.at[h], video_slot(h), video_send.at[4], video_recv.at[h], sibling
        )
        for h in range(2)
    ]

    def keep_video(h):
        @pl.when(diag)
        def _():
            local(NV.at[h], video_slot(h), video_recv.at[h]).start()

        @pl.when(not_diag)
        def _():
            own_chip[h].start()

    def send_lower():
        keep_video(0)
        for k in (2, 1, 3):
            video_x(k).start()

    def send_upper():
        keep_video(1)
        for k in (2, 1, 3):
            video_y(k).start()

    def lower_on(k):
        ref = XG.at[0, :, yl]
        return remote(ref, ref, video_send.at[2], video_recv.at[2], at_core(x, (y + k) % 4, c))

    def upper_on(k):
        ref = XG.at[1, x]
        return remote(ref, ref, video_send.at[3], video_recv.at[3], at_core((x + k) % 4, y, c))

    def pass_upper_on():
        ref = XG.at[1, 0]
        local(ref, ref, video_recv.at[1]).wait()
        for k in (2, 1, 3):
            upper_on(k).start()

    def pass_lower_on():
        @pl.when(diag)
        def _():
            ref = XG.at[0, pl.ds(0, 2)]
            local(ref, ref, video_recv.at[0]).wait()
            for k in (2, 1, 3):
                lower_on(k).start()

    def video_wait():
        ref = XG.at[1, pl.ds(0, 3)]
        local(ref, ref, video_recv.at[3]).wait()

        @pl.when(diag)
        def _():
            ref = XG.at[0, pl.ds(0, 2)]
            local(ref, ref, video_recv.at[2]).wait()

        @pl.when(not_diag)
        def _():
            ref = XG.at[0]
            local(ref, ref, video_recv.at[2]).wait()

    PROMPTS, SUMS, TEXT = range(3)

    def send_prompt(k):
        device = (c * 8 + z, ((x + k // 2) % 4) * 4 + ((yl + k % 2) % 2) * 2 + x // 2)
        return remote(SEL, PG.at[head_block], group_send.at[PROMPTS], group_recv.at[PROMPTS], device)

    half_chosen = PG.at[pl.ds(pl.multiple_of(c * 8, 8), 8)]
    pass_chosen = remote(half_chosen, half_chosen, prompt_sem.at[2], prompt_sem.at[3], sibling)

    def pass_chosen_on():
        local(half_chosen, half_chosen, group_recv.at[PROMPTS]).wait()
        pass_chosen.start()

    def spread(first, last, make):
        def step(k, carry):
            make(k).start()
            return carry

        lax.fori_loop(first, last, step, 0)

    def first_send(copy, copy_local, group):
        @pl.when(diag)
        def _():
            copy_local.start()

        @pl.when(jnp.logical_not(diag))
        def _():
            copy.start()

    prompt0 = remote(
        SEL,
        PG.at[head_block],
        group_send0.at[PROMPTS],
        group_recv.at[PROMPTS],
        (c * 8 + z, x * 4 + yl * 2 + x // 2),
    )
    chosen_here = jnp.logical_and(diag, c == x // 2)

    def send_prompts():
        ring_wait(PROMPT, z)
        ref = PB.at[c * 8 + z]

        def step(k, carry):
            remote(
                ref, ref, ring_send.at[PROMPT], sib_recv.at[PROMPT], (yh * 8 + (z + k) % 8, seq)
            ).start()
            return carry

        lax.fori_loop(1, 8, step, 0)

    half_prompts = PB.at[pl.ds(pl.multiple_of(c * 8, 8), 8)]
    pass_prompts = remote(half_prompts, half_prompts, prompt_sem.at[0], prompt_sem.at[1], sibling)

    def pass_prompts_on():
        ref = PB.at[pl.ds(0, 7)]
        local(ref, ref, sib_recv.at[PROMPT]).wait()
        pass_prompts.start()

    def choose_prompt():
        pass_prompts.wait_recv()
        local(info, info, info_sem).wait()
        wanted = info[0:1, 0:1]

        def pick(i, total):
            return total + jnp.where(wanted == i, PB[i].astype(F32), 0.0)

        SEL[...] = lax.fori_loop(0, 16, pick, jnp.zeros(SEL.shape, F32)).astype(BF)

        @pl.when(chosen_here)
        def _():
            local(SEL, PG.at[head_block], group_recv.at[PROMPTS]).start()

        @pl.when(jnp.logical_not(chosen_here))
        def _():
            prompt0.start()

        spread(1, 8, send_prompt)

    def norm_rows(i, carry):
        rows = PG[pl.ds(2 * i, 2)].astype(F32).reshape(16, PG.shape[2])
        FN[pl.ds(pl.multiple_of(i * 16, 16), 16), :] = rms_norm(rows, ffn_gain_ref[...]).astype(BF)
        return carry

    def ffn_norm():
        pass_chosen.wait_recv()
        lax.fori_loop(0, 8, norm_rows, 0)

    def ffn_project(weights, acc, copy):
        copy.wait()

        def step(i, total):
            at = pl.ds(pl.multiple_of(i * 512, 512), 512)
            return total + jnp.dot(FN[:, at], weights[at, :], preferred_element_type=F32)

        acc[...] = lax.fori_loop(0, 8, step, jnp.zeros(acc.shape, F32))

    def ffn_gate():
        ffn_project(gate_ref, gate_acc, ffn_copies[0])

    def ffn_up():
        ffn_project(up_ref, up_acc, ffn_copies[1])
        hidden[...] = (jax.nn.gelu(gate_acc[...], approximate=True) * up_acc[...]).astype(BF)

    def down_proj(i, carry):
        at = pl.ds(pl.multiple_of(i * 256, 256), 256)
        part = jnp.dot(hidden[...], down_ref[:, at], preferred_element_type=F32)
        FP[:, :, :, at] = part.reshape(8, 2, 8, 256).astype(BF)
        return carry

    pass_sums = remote(FP.at[:, 1 - c], FS, prompt_sem.at[4], prompt_sem.at[5], sibling)
    own_chip_index = seq // 2

    def send_sums(k):
        to = ((x + k // 2) % 4) * 2 + (yl + k % 2) % 2
        return remote(
            FQ.at[to], FR.at[own_chip_index], group_send.at[SUMS], group_recv.at[SUMS], (vid, to * 2 + c)
        )

    def ffn_down():
        ffn_copies[2].wait()
        lax.fori_loop(0, 16, down_proj, 0)
        pass_sums.start()

    def ffn_sums():
        pass_sums.wait_recv()

        def step(i, carry):
            FQ[i] = (FP[i, c].astype(F32) + FS[i].astype(F32)).astype(BF)
            return carry

        lax.fori_loop(0, 8, step, 0)
        local(FQ.at[own_chip_index], FR.at[own_chip_index], group_recv.at[SUMS]).start()
        spread(1, 8, send_sums)

    def send_text(k):
        return remote(TX, TG.at[seq], group_send.at[TEXT], group_recv.at[TEXT], to_chip(k))

    text0 = remote(TX, TG.at[seq], group_send0.at[TEXT], group_recv.at[TEXT], to_chip(0))

    def text_rows():
        local(FR, FR, group_recv.at[SUMS]).wait()
        encoded = lax.fori_loop(
            0, 8, lambda i, total: total + FR[i].astype(F32), jnp.zeros(TX.shape, F32)
        )
        encoded = PG[seq].astype(F32) + encoded
        TX[...] = rms_norm(encoded, final_gain_ref[...]).astype(BF)
        first_send(text0, local(TX, TG.at[seq], group_recv.at[TEXT]), TEXT)
        spread(1, 16, send_text)

    def video_rows(j):
        at = pl.ds(pl.multiple_of((j % 4) * 512, 512), 512)
        return XG[j // 4, :, :, :, :, at].reshape(512, 512)

    def project(w, acc, result):
        sibling_wait(w)
        acc[...] = jnp.zeros_like(acc)

        def step(j, carry):
            weights = W[w, pl.ds(2 * j, 2)].reshape(512, 256)
            acc[...] += jnp.dot(video_rows(j), weights, preferred_element_type=F32)
            return carry

        lax.fori_loop(0, 8, step, 0)
        result[pl.ds(0, 512), :] = acc[...].astype(BF)

    def text_key_value(j, carry):
        at = pl.ds(pl.multiple_of(j * 256, 256), 256)
        rows = TG[:, :, at].astype(F32).reshape(128, 256).astype(BF)
        key_sum, value_sum = carry
        key_sum = key_sum + jnp.dot(rows, W[TK, j], preferred_element_type=F32)
        value_sum = value_sum + jnp.dot(rows, W[TV, j], preferred_element_type=F32)
        return key_sum, value_sum

    def text_projections():
        local(TG, TG, group_recv.at[TEXT]).wait()
        sibling_wait(TK)
        sibling_wait(TV)
        zero = jnp.zeros((128, 256), F32)
        text_key, text_value = lax.fori_loop(0, 16, text_key_value, (zero, zero))
        keys[pl.ds(512, 128), :] = text_key.astype(BF)
        values[pl.ds(512, 128), :] = text_value.astype(BF)

    def attended_x(part, xk):
        ref = AX.at[x, part]
        return remote(ref, ref, out_send.at[0], out_recv.at[part], at_core(xk, y, c))

    def out_y(part, k):
        return remote(
            SB.at[pl.ds(part * 4 + k * 2, 2)],
            YR.at[(y + 3 - (c * 2 + k)) % 4, pl.ds(part * 2, 2)],
            out_send.at[1 + k],
            out_recv.at[4 + part],
            at_core(x, c * 2 + k, c),
        )

    def sum_y(xk, core):
        return remote(
            YS.at[xk * 2 + core], RR.at[x], out_send.at[3], out_recv.at[8], at_core(xk, y, core)
        )

    def attention_probs(first, last):
        position = lax.broadcasted_iota(jnp.int32, (1, 640), 1)
        live = position < jnp.where(position < 512, info[1:2, 0:1], info[2:3, 0:1] + 512)

        def step(i, carry):
            part = (x + 1 + i) % 4
            rows = pl.ds(pl.multiple_of(part * 128, 128), 128)
            for h in range(2):
                lanes = pl.ds(h * HD, HD)
                scores = lax.dot_general(
                    queries[rows, lanes], keys[:, lanes], (((1,), (1,)), ((), ())), preferred_element_type=F32
                )
                scores = jnp.where(live, scores * HD ** (-0.5), -1e30)
                e = jnp.exp(scores - jnp.max(scores, axis=-1, keepdims=True))
                probs[part, h] = (e / jnp.sum(e, axis=-1, keepdims=True)).astype(BF)
            return carry

        lax.fori_loop(first, last, step, 0)

    def attend(part, carry):
        for h in range(2):
            lanes = pl.ds(h * HD, HD)
            AX[x, part, :, lanes] = jnp.dot(
                probs[part, h], values[:, lanes], preferred_element_type=F32
            ).astype(BF)
        return carry

    def attend_all():
        lax.fori_loop(0, 4, attend, 0)

        def step(i, carry):
            for k in (2, 1, 3):
                xk = (x + k) % 4
                attended_x((xk + 1 + i) % 4, xk).start()
            return carry

        lax.fori_loop(0, 4, step, 0)

    def project_part(i, carry):
        part = (x + 1 + i) % 4
        ref = AX.at[pl.ds(0, 3), 0]
        local(ref, ref, out_recv.at[part]).wait()
        rows = [jnp.concatenate([AX[2 * j, part], AX[2 * j + 1, part]], axis=1) for j in range(2)]
        for m in range(4):
            total = jnp.zeros((128, 256), F32)
            for j in range(2):
                weights = jnp.concatenate(
                    [OX[j * 8 + 2 * m + i].reshape(512, 128) for i in range(2)], axis=1
                )
                total = total + jnp.dot(rows[j], weights, preferred_element_type=F32)
            SB[pl.ds(part * 4, 4), :, pl.ds(m * 256, 256)] = total.reshape(4, 32, 256).astype(BF)
        for k in range(2):

            @pl.when(y != c * 2 + k)
            def _():
                out_y(part, k).start()

        return carry

    def sum_part(i, carry):
        part = (x + 1 + i) % 4
        ref = YR.at[pl.ds(0, 3), pl.ds(0, 2)]
        local(ref, ref, out_recv.at[4 + part]).wait()
        for step in range(2):
            core = (c + 1 + step) % 2
            total = SB[part * 4 + yl * 2 + core].astype(F32)
            for j in range(3):
                total = total + YR[j, part * 2 + core].astype(F32)
            YS[part * 2 + core] = total.astype(BF)
            to_here = jnp.logical_and(part == x, core == c)

            @pl.when(jnp.logical_not(to_here))
            def _():
                sum_y(part, core).start()

            @pl.when(to_here)
            def _():
                local(YS.at[part * 2 + core], RR.at[x], out_recv.at[8]).start()

        return carry

    send_lower()
    swap(TK)
    own(PROMPT)
    swap(TV)
    hop(PROMPT, 1)
    send_upper()
    swap(Q)
    own(TK)
    hop(PROMPT, 2)
    swap(K)
    hop(PROMPT, 3)
    own(TV)
    swap(O)
    hop(PROMPT, 4)
    pass_prompts.start()
    own(Q)
    swap(V)
    own(K)
    hop(TK, 1)
    choose_prompt()
    hop(TV, 1)
    hop(Q, 1)
    hop(K, 1)
    own(O)
    own(V)
    pass_chosen_on()
    pass_upper_on()
    pass_lower_on()
    ffn_norm()
    ffn_gate()
    ffn_up()
    hop(TK, 2)
    hop(TV, 2)
    hop(Q, 2)
    hop(K, 2)
    hop(O, 1)
    ffn_down()
    hop(V, 1)
    hop(TK, 3)
    ffn_sums()
    hop(TV, 3)
    hop(Q, 3)
    hop(K, 3)
    hop(O, 2)
    hop(V, 2)
    text_rows()
    hop(TK, 4)
    hop(TV, 4)
    hop(Q, 4)
    hop(K, 4)
    video_wait()
    project(Q, q_acc, queries)
    hop(O, 3)
    hop(V, 3)
    project(K, k_acc, keys)
    hop(V, 4)
    text_projections()
    attention_probs(0, 4)
    project(V, v_acc, values)
    hop(O, 4)
    attend_all()
    sibling_wait(O)
    lax.fori_loop(0, 4, project_part, 0)

    @pl.when(diag)
    def _():
        lax.fori_loop(0, 4, sum_part, 0)

    local(RR, RR, out_recv.at[8]).wait()
    row_position = seq * 32 + lax.broadcasted_iota(jnp.int32, (32, 1), 0)
    row_live = row_position < length_ref[0]

    for j in range(4):
        for i in range(8):
            at = pl.ds((j // 2) * 2048 + i * 256 + (j % 2) * 128, 128)
            total = RR[j, :, pl.ds(i * 128, 128)].astype(F32)
            updated = video_ref[0, :, at].astype(F32) + jnp.where(row_live, total, 0.0)
            out_ref[0, :, at] = updated.astype(BF)

    for w in (TK, TV, Q, K, V, PROMPT):
        swap_copy(w).wait_send()
    local(OX.at[0], OX.at[0], swap_send.at[O]).wait()
    info_copy.wait_send()

    @pl.when(jnp.logical_not(diag))
    def _():
        text0.wait_send()
        both = XG.at[0, 0, 0]
        local(both, both, video_send.at[4]).wait()

    pass_prompts.wait_send()
    for w in range(7):
        ref = slot(w, pl.ds(0, 7 if w == PROMPT else 15))
        local(ref, ref, ring_send.at[w]).wait()
    @pl.when(jnp.logical_not(chosen_here))
    def _():
        prompt0.wait_send()

    pass_chosen.wait_send()
    pass_sums.wait_send()
    for group, buffer in ((PROMPTS, PG), (SUMS, FR), (TEXT, TG)):
        ref = buffer.at[pl.ds(0, 15 if group == TEXT else 7)]
        local(ref, ref, group_send.at[group]).wait()
    for sem in (video_send.at[0], video_send.at[1]):
        ref = XG.at[0, pl.ds(0, 3), 0, 0]
        local(ref, ref, sem).wait()
    ref = XG.at[0, pl.ds(0, 3)]
    local(ref, ref, video_send.at[3]).wait()
    ref = AX.at[pl.ds(0, 3)]
    local(ref, ref, out_send.at[0]).wait()
    for k in range(2):

        @pl.when(y != c * 2 + k)
        def _():
            ref = SB.at[pl.ds(0, 8)]
            local(ref, ref, out_send.at[1 + k]).wait()

    @pl.when(diag)
    def _():
        ref = XG.at[:, pl.ds(0, 3)]
        local(ref, ref, video_send.at[2]).wait()
        ref = YS.at[pl.ds(0, 7)]
        local(ref, ref, out_send.at[3]).wait()


def block(
    video,
    video_length,
    prompt,
    prompt_length,
    prompt_choice,
    ffn_gain,
    ffn_gate,
    ffn_up,
    ffn_down,
    final_gain,
    video_gain,
    w_query,
    w_key,
    w_value,
    w_text_key,
    w_text_value,
    w_out,
):
    smem = pl.BlockSpec(memory_space=pltpu.SMEM)
    vmem = pl.BlockSpec(memory_space=pltpu.VMEM)
    hbm = pl.BlockSpec(memory_space=pl.ANY)
    dma = pltpu.SemaphoreType.DMA
    width, half, quarter = 4096, 2048, 1024
    return pl.pallas_call(
        kernel,
        out_shape=jax.ShapeDtypeStruct(video.shape, video.dtype),
        in_specs=[smem] * 3 + [vmem] * 5 + [hbm] * 9,
        out_specs=vmem,
        scratch_shapes=[
            pltpu.VMEM((5, 16, 256, 256), BF),
            pltpu.VMEM((16, 8, width), BF),
            pltpu.VMEM((8, width), BF),
            pltpu.VMEM((16, 8, width), BF),
            pltpu.VMEM((128, width), BF),
            pltpu.VMEM(ffn_gate.shape, BF),
            pltpu.VMEM(ffn_up.shape, BF),
            pltpu.VMEM(ffn_down.shape, BF),
            pltpu.VMEM((128, 384), F32),
            pltpu.VMEM((128, 384), F32),
            pltpu.VMEM((128, 384), BF),
            pltpu.VMEM((8, 2, 8, width), BF),
            pltpu.VMEM((8, 8, width), BF),
            pltpu.VMEM((8, 8, width), BF),
            pltpu.VMEM((8, 8, width), BF),
            pltpu.VMEM((8, width), BF),
            pltpu.VMEM((16, 8, width), BF),
            pltpu.VMEM((2, 32, half), BF),
            pltpu.VMEM((2, 4, 2, 2, 32, half), BF),
            pltpu.VMEM((512, 256), F32),
            pltpu.VMEM((512, 256), F32),
            pltpu.VMEM((512, 256), F32),
            pltpu.VMEM((512, 256), BF),
            pltpu.VMEM((4, 2, 128, 640), BF),
            pltpu.VMEM((640, 256), BF),
            pltpu.VMEM((640, 256), BF),
            pltpu.VMEM((4, 4, 128, 256), BF),
            pltpu.VMEM((16, 2, 256, 128), BF),
            pltpu.VMEM((16, 32, quarter), BF),
            pltpu.VMEM((3, 8, 32, quarter), BF),
            pltpu.VMEM((8, 32, quarter), BF),
            pltpu.VMEM((4, 32, quarter), BF),
            pltpu.VMEM((8, 128), jnp.int32),
            pltpu.VMEM((8, 128), jnp.int32),
            dma((3,)),
            dma((7, 8)),
            dma((7,)),
            dma((8,)),
            dma((7,)),
            dma,
            dma((3,)),
            dma((3,)),
            dma((3,)),
            dma((6,)),
            dma((4,)),
            dma((5,)),
            dma((9,)),
            dma((5,)),
        ],
        compiler_params=pltpu.CompilerParams(
            collective_id=0, has_side_effects=True, vmem_limit_bytes=58 * 1024 * 1024
        ),
        name="joint_attention",
    )(
        video_length,
        prompt_length,
        prompt_choice,
        video,
        prompt,
        ffn_gain.reshape(1, -1),
        final_gain.reshape(1, -1),
        video_gain.reshape(1, -1),
        ffn_gate,
        ffn_up,
        ffn_down,
        w_text_key,
        w_text_value,
        w_query,
        w_key,
        w_value,
        w_out,
    )


def solution(mesh):
    in_specs = (
        P("vid", "seq", None),
        P("vid"),
        P("vid", "seq", None),
        P(),
        P("vid"),
        P(),
        P(None, "seq"),
        P(None, "seq"),
        P("seq", None),
        P(),
        P(),
        P("vid", "seq"),
        P("vid", "seq"),
        P("vid", "seq"),
        P("vid", "seq"),
        P("vid", "seq"),
        P("seq", "vid"),
    )
    out_specs = P("vid", "seq", None)
    return jax.shard_map(block, mesh=mesh, in_specs=in_specs, out_specs=out_specs, check_vma=False)
```
